32 devices in a mesh: seq: 4 (over z), batch: 4 (over y, x), tp: 2 (over core).
Axes of the slice: x: 2, y: 2, z: 4, core: 2. Of those that a mesh axis runs over, the one named last changes fastest.
Arguments:
- pre_q: bfloat16 [4, 512, 4096], P('batch', 'seq', 'tp'), may hold values from -40 to 40
- pre_k: bfloat16 [4, 512, 512], P('batch', 'seq', 'tp'), may hold values from -40 to 40
- pre_v: bfloat16 [4, 512, 512], P('batch', 'seq', 'tp'), may hold values from -12 to 12
- owner_map: int32 [4, 32, 1], P('batch', 'seq'), may hold values from 0 to 3; in each aligned block of 8 rows (0 to 7, 8 to 15, ..., all dimensions but the last counted through in order) at most 4 rows name the same one
- cache_k: bfloat16 [32, 64, 512], P('batch', 'seq', 'tp'), may hold values from -6 to 6
- cache_v: bfloat16 [32, 64, 512], P('batch', 'seq', 'tp'), may hold values from -12 to 12
- tables: int32 [8, 16], P('batch', 'seq'), may hold values from 0 to 7, as said below
- lengths: int32 [8], P('batch'), may hold values from 1 to 256, 1024 in all
- dec_q: float32 [8, 3, 4096], P('batch', None, 'tp'), may hold values from -40 to 40
- dec_k: float32 [8, 3, 512], P('batch', None, 'tp'), may hold values from -40 to 40
- dec_v: float32 [8, 3, 512], P('batch', None, 'tp'), may hold values from -12 to 12
- w_out: bfloat16 [4096, 8192], P('tp', 'seq'), may hold values from -0.09375 to 0.09375
Outputs:
- pre_out: bfloat16 [4, 512, 4096], P('batch', 'seq', 'tp')
- dec_out: float32 [8, 3, 8192], P('batch', None, 'seq')
The draws below stay inside these ranges and needn't reach their ends.
Inputs may be any that keep to these rules, and one draw needn't show every extreme that they name: `owner_map`: in each aligned block of 8 rows (the pages of one index of seq of one span) no owner is named more than 4 times. `tables`: within one owner's 2 requests and one index of seq, the 8 entries are distinct.
All inputs are finite; a program needn't handle non-finite values. No bound on the sum of `lengths` on one device may be relied on, other than what follows from the above.
Results may differ from the reference program's by a relative error of at most 0.0033.
Values may be sent and summed in bfloat16 or wider, within the bound.
A program may use at most 64 MiB of HBM per device.

```python
import math
import jax
import jax.numpy as jnp
import numpy as np
from jax import lax

HD = 128
QH = 32
KVH = 4
D = 8192
PAGE = 16
NEW = 3
R_DEV = 2
TBL = 4
SEQ_LEN = 512
PG_DEV = 8
MOST = 4
REQS = 8
POOL = 8
CTX = 256
N_SEQ = 4
N_BATCH = 4


def draw_pre_k(key, part):
    key = jax.random.fold_in(key, 21)
    return jnp.clip(jax.random.normal(key, (N_BATCH, SEQ_LEN, KVH * HD), jnp.float32), -5.0, 5.0).astype(jnp.bfloat16)


def draw_pre_q(key, part):
    key = jax.random.fold_in(key, 22)
    return (2.0 * jnp.clip(jax.random.normal(key, (N_BATCH, SEQ_LEN, QH * HD), jnp.float32), -5.0, 5.0)).astype(jnp.bfloat16)


def draw_dec_k(key, part):
    key = jax.random.fold_in(key, 31)
    return jnp.clip(jax.random.normal(key, (REQS, NEW, KVH * HD), jnp.float32), -5.0, 5.0)


def draw_dec_q(key, part):
    key = jax.random.fold_in(key, 32)
    return 2.0 * jnp.clip(jax.random.normal(key, (REQS, NEW, QH * HD), jnp.float32), -5.0, 5.0)


def draw_tables(key, part):
    key = jax.random.fold_in(key, 5)
    split_keys = jax.random.split(key, N_BATCH * N_SEQ)
    orders = jax.vmap(lambda single: jax.random.permutation(single, POOL))(split_keys).astype(jnp.int32)
    orders = orders.reshape(N_BATCH, N_SEQ, R_DEV, TBL).transpose(0, 2, 1, 3)
    return orders.reshape(REQS, N_SEQ * TBL)


def block_scale(key, shape, shards, low, high):
    def one(axis_at, blocks):
        steps = jax.random.uniform(jax.random.fold_in(jax.random.fold_in(key, 6), axis_at), (blocks,), jnp.float32, low / len(shards), high / len(shards))
        return jnp.repeat(jnp.exp(steps), shape[axis_at] // blocks).reshape((-1,) + (1,) * (len(shape) - axis_at - 1))

    factor_of = one(*shards[0])
    for cut in shards[1:]:
        factor_of = factor_of * one(*cut)
    return factor_of


def profile(count, total, reach, slope):
    portions = [(1 << 20) // math.isqrt(grade ** slope) + 1 for grade in range(2, count + 1)]
    rest, holding = total - reach - (count - 1), [1] * (count - 1)
    while rest > 0:
        candidates = [i for i in range(count - 1) if holding[i] < reach]
        whole, budget = sum([portions[i] for i in candidates]), rest
        for i in candidates:
            more = min(reach - holding[i], max(1, budget * portions[i] // whole), rest)
            holding[i] = holding[i] + more
            rest = rest - more
    return np.array([reach] + holding)


def ragged_sizes(stream_key, count, total, most, lean):
    if count == 2:
        one = jax.random.randint(stream_key, (), max(1, total - most), min(most, total - 1) + 1)
        return jnp.stack([one, total - one])
    sizes = jnp.asarray(profile(count, total, most, lean), jnp.int32)
    couples = (count - 1) // 2
    donor, receiver = sizes[1:1 + 2 * couples:2], sizes[2:2 + 2 * couples:2]
    room = jnp.minimum(donor - 1, most - receiver)
    moved = jax.random.randint(jax.random.fold_in(stream_key, 1), (couples,), 0, 1 << 20) % (room + 1)
    sizes = sizes.at[1:1 + 2 * couples:2].set(donor - moved).at[2:2 + 2 * couples:2].set(receiver + moved)
    return sizes[jax.random.permutation(jax.random.fold_in(stream_key, 2), count)]


def shared_out(rng, own, number, rows, number_of, top, most, skew):
    sequence = jax.random.permutation(rng, number_of)
    crowded, usual = load_shares(number_of, rows * top, most, skew, True), load_shares(number_of, rows * top, most, skew, False)
    places = jnp.arange(number_of)

    def named(sizes, rotation):
        used = int((sizes > 0).sum())
        fixed = max(1, used // 4)
        passed = fixed + (places - fixed + rotation * (used - fixed)) % max(1, number_of - fixed)
        return jnp.zeros((number_of,), jnp.int32).at[sequence[jnp.where(places < fixed, places, passed)]].set(jnp.asarray(sizes, jnp.int32))

    sizes = jnp.where(number % 4 == 0, named(crowded, number // 4), named(usual, number - number // 4 - 1))
    mixed = jax.random.permutation(jax.random.fold_in(own, 3), number_of)
    donor, sink = mixed[0:number_of // 2 * 2:2], mixed[1:number_of // 2 * 2:2]
    room = jnp.minimum(sizes[donor] - 1, most - sizes[sink]) // 2
    room = jnp.where((donor == sequence[0]) | (sink == sequence[0]) | (sizes[sink] == 0), 0, jnp.maximum(room, 0))
    passed = jax.random.randint(jax.random.fold_in(own, 4), (number_of // 2,), 0, 1 << 20) % (room + 1)
    sizes = sizes.at[donor].add(-passed).at[sink].add(passed)
    labels = jnp.searchsorted(jnp.cumsum(sizes), jnp.arange(rows * top), side="right").astype(jnp.int32)
    grid = labels.reshape(top, rows).T
    grid = grid[jax.random.permutation(jax.random.fold_in(own, 1), rows)]
    rotation = jax.random.randint(jax.random.fold_in(own, 2), (rows, 1), 0, top)
    return jnp.take_along_axis(grid, (jnp.arange(top)[None, :] + rotation) % top, axis=1)


def load_shares(number_of, total, most, lean, full):
    portions = [(1 << 20) // math.isqrt(rank ** lean) + 1 for rank in range(1, number_of + 1)]
    largest = most if full else min(most, max(-(-total // number_of), total * portions[0] // sum(portions)))
    least = 1 if total - largest >= number_of - 1 else 0
    counts, rest = [largest] + [least] * (number_of - 1), total - largest - least * (number_of - 1)
    while rest > 0:
        free = [i for i in range(1, number_of) if counts[i] < largest] or [i for i in range(1, number_of) if counts[i] < most]
        whole, left = sum([portions[i] for i in free]), rest
        for i in free:
            addition = min(most - counts[i], max(1, left * portions[i] // whole), rest)
            counts[i] = counts[i] + addition
            rest = rest - addition
    return np.array(counts)


def normal_values(stream_key, dims, spread, reach, shards=(), held_as=jnp.bfloat16):
    result = jax.random.normal(stream_key, dims, jnp.float32) * spread
    if len(shards) > 0:
        result = block_scale(stream_key, dims, shards, -0.22, 0.18) * result
    return jnp.clip(result, min=-reach, max=reach).astype(held_as)


def setup_inputs(seed: int = 0) -> dict:
    keys = jax.random.split(jax.random.key(seed), 13)
    pre_q = draw_pre_q(jax.random.fold_in(keys[12], 71), 0)
    pre_k = draw_pre_k(jax.random.fold_in(keys[12], 71), 0)
    pre_v = normal_values(keys[2], (N_BATCH, SEQ_LEN, KVH * HD), 2.0, 12.0, ((0, 4), (1, 4), (2, 2)))
    owner_map_keys = jax.random.split(jax.random.fold_in(keys[3], 1), N_BATCH * (N_SEQ * PG_DEV) // PG_DEV)
    owner_map_turns = jax.random.permutation(jax.random.fold_in(keys[3], 3), N_BATCH * (N_SEQ * PG_DEV) // PG_DEV)
    owner_map = jax.vmap(lambda own, number: shared_out(jax.random.fold_in(keys[3], 2), own, number, PG_DEV, N_BATCH, 1, MOST, 2))(owner_map_keys, owner_map_turns).reshape((N_BATCH, N_SEQ * PG_DEV, 1))
    cache_k = normal_values(keys[4], (REQS * TBL, N_SEQ * PAGE, KVH * HD), 1.0, 6.0, ((0, 4), (1, 4), (2, 2)))
    cache_v = normal_values(keys[5], (REQS * TBL, N_SEQ * PAGE, KVH * HD), 2.0, 12.0, ((0, 4), (1, 4), (2, 2)))
    tables = draw_tables(jax.random.fold_in(keys[12], 71), 0)
    lengths = ragged_sizes(keys[7], REQS, REQS * CTX // 2, CTX, 2).astype(jnp.int32)
    dec_q = draw_dec_q(jax.random.fold_in(keys[12], 71), 0)
    dec_k = draw_dec_k(jax.random.fold_in(keys[12], 71), 0)
    dec_v = normal_values(keys[10], (REQS, NEW, KVH * HD), 2.0, 12.0, ((0, 4), (2, 2)), jnp.float32)
    w_out = normal_values(keys[11], (QH * HD, D), (QH * HD) ** -0.5, 0.09375, ((0, 2), (1, 4)))
    return dict(pre_q=pre_q, pre_k=pre_k, pre_v=pre_v, owner_map=owner_map, cache_k=cache_k, cache_v=cache_v, tables=tables, lengths=lengths, dec_q=dec_q, dec_k=dec_k, dec_v=dec_v, w_out=w_out)


highest = lax.Precision.HIGHEST
floor_score = -1e30


def prefill_span(inputs):
    queries, key_rows, value_rows = inputs
    group_size = QH // KVH
    scaling = HD ** -0.5
    q_all = queries.astype(jnp.float32).reshape(SEQ_LEN, KVH, group_size, HD)
    k_all = key_rows.astype(jnp.float32).reshape(SEQ_LEN, KVH, HD)
    v_all = value_rows.astype(jnp.float32).reshape(SEQ_LEN, KVH, HD)
    block_rows = min(512, SEQ_LEN)
    pieces = []
    for block_id in range(SEQ_LEN // block_rows):
        end_row = (block_id + 1) * block_rows
        query_block = q_all[block_id * block_rows:end_row]
        scores = jnp.einsum("qkgd,skd->kgqs", query_block, k_all[:end_row], precision=highest) * scaling
        query_pos = block_id * block_rows + jnp.arange(block_rows, dtype=jnp.int32)
        visible = jnp.arange(end_row, dtype=jnp.int32)[None, :] <= query_pos[:, None]
        masked = jnp.where(visible, scores, floor_score)
        row_peak = jnp.max(masked, axis=-1, keepdims=True)
        weights = jnp.where(visible, jnp.exp(scores - row_peak), 0.0)
        row_total = jnp.sum(weights, axis=-1)
        rounded = lax.optimization_barrier(weights.astype(jnp.bfloat16)).astype(jnp.float32)
        mixture = jnp.einsum("kgqs,skd->qkgd", rounded, v_all[:end_row], precision=highest)
        mixture = mixture / jnp.transpose(row_total, (2, 0, 1))[..., None]
        pieces.append(mixture.reshape(block_rows, QH * HD).astype(jnp.bfloat16))
    return jnp.concatenate(pieces, axis=0)


def reference(pre_q, pre_k, pre_v, owner_map, cache_k, cache_v, tables, lengths, dec_q, dec_k, dec_v, w_out):
    pre_out = lax.map(prefill_span, (pre_q, pre_k, pre_v))
    group_size = QH // KVH
    scaling = HD ** -0.5
    token_keys = pre_k.reshape(N_BATCH * SEQ_LEN, KVH, HD)
    token_values = pre_v.reshape(N_BATCH * SEQ_LEN, KVH, HD)
    token_owner = jnp.repeat(owner_map.reshape(-1), PAGE).astype(jnp.int32)
    capacity = min(N_BATCH * SEQ_LEN, N_BATCH * N_SEQ * MOST * PAGE)
    positions = ((jnp.arange(TBL, dtype=jnp.int32)[None, :, None] * N_SEQ
                  + jnp.arange(N_SEQ, dtype=jnp.int32)[:, None, None]) * PAGE
                 + jnp.arange(PAGE, dtype=jnp.int32)[None, None, :]).reshape(-1)
    causal = (jnp.arange(NEW, dtype=jnp.int32)[None, :] <= jnp.arange(NEW, dtype=jnp.int32)[:, None])[None, :, None, None, :]

    def decode_owner(inputs):
        owner, queries, table, request_len, pool_keys, pool_values, new_keys, new_values = inputs
        query_rows = queries.reshape(R_DEV, NEW, KVH, group_size, HD)
        owner_order = jnp.argsort((token_owner != owner).astype(jnp.int32), stable=True)[:capacity]
        received = token_owner[owner_order] == owner
        recv_keys = token_keys[owner_order].astype(jnp.float32)
        recv_values = token_values[owner_order].astype(jnp.float32)
        slots = table.reshape(R_DEV, N_SEQ, TBL)
        seq_ids = jnp.arange(N_SEQ, dtype=jnp.int32)[None, :, None]
        pools_k = pool_keys.reshape(POOL, N_SEQ, PAGE, KVH, HD).transpose(1, 0, 2, 3, 4).astype(jnp.float32)
        pools_v = pool_values.reshape(POOL, N_SEQ, PAGE, KVH, HD).transpose(1, 0, 2, 3, 4).astype(jnp.float32)
        cached_k = pools_k[seq_ids, slots].reshape(R_DEV, N_SEQ * TBL * PAGE, KVH, HD)
        cached_v = pools_v[seq_ids, slots].reshape(R_DEV, N_SEQ * TBL * PAGE, KVH, HD)
        cached_live = (positions[None, :] < request_len[:, None])[:, None, None, None, :]
        score_cache = jnp.einsum("rnkgd,rtkd->rnkgt", query_rows, cached_k, precision=highest) * scaling
        score_recv = jnp.einsum("rnkgd,tkd->rnkgt", query_rows, recv_keys, precision=highest) * scaling
        score_new = jnp.einsum("rnkgd,rjkd->rnkgj", query_rows, new_keys, precision=highest) * scaling
        row_peak = jnp.maximum(jnp.max(jnp.where(cached_live, score_cache, floor_score), axis=-1),
                               jnp.max(jnp.where(received, score_recv, floor_score), axis=-1))
        row_peak = jnp.maximum(row_peak, jnp.max(jnp.where(causal, score_new, floor_score), axis=-1))
        weight_cache = jnp.where(cached_live, jnp.exp(score_cache - row_peak[..., None]), 0.0)
        weight_recv = jnp.where(received, jnp.exp(score_recv - row_peak[..., None]), 0.0)
        weight_new = jnp.where(causal, jnp.exp(score_new - row_peak[..., None]), 0.0)
        row_total = jnp.sum(weight_cache, axis=-1) + jnp.sum(weight_recv, axis=-1) + jnp.sum(weight_new, axis=-1)
        mixture = jnp.einsum("rnkgt,rtkd->rnkgd", weight_cache, cached_v, precision=highest)
        mixture = mixture + jnp.einsum("rnkgt,tkd->rnkgd", weight_recv, recv_values, precision=highest)
        mixture = mixture + jnp.einsum("rnkgj,rjkd->rnkgd", weight_new, new_values, precision=highest)
        return (mixture / row_total[..., None]).reshape(R_DEV * NEW, QH * HD)

    attention = lax.map(decode_owner, (
        jnp.arange(N_BATCH, dtype=jnp.int32),
        dec_q.reshape(N_BATCH, R_DEV, NEW, QH * HD),
        tables.reshape(N_BATCH, R_DEV, N_SEQ * TBL),
        lengths.reshape(N_BATCH, R_DEV),
        cache_k.reshape(N_BATCH, POOL, N_SEQ * PAGE, KVH * HD),
        cache_v.reshape(N_BATCH, POOL, N_SEQ * PAGE, KVH * HD),
        dec_k.reshape(N_BATCH, R_DEV, NEW, KVH, HD),
        dec_v.reshape(N_BATCH, R_DEV, NEW, KVH, HD)))
    dec_out = jnp.dot(attention.reshape(REQS * NEW, QH * HD), w_out.astype(jnp.float32), precision=highest)
    return pre_out, dec_out.reshape(REQS, NEW, D)
```

```python
import functools

import jax
import jax.numpy as jnp
from jax import lax
from jax.experimental import pallas as pl
from jax.experimental.pallas import tpu as pltpu
from jax.sharding import PartitionSpec as P

HD = 128
MOST = 4
ROWS = 8
LANES = 128
floor_score = -1e30


def halves(x):
    high = x.astype(jnp.bfloat16)
    low = (x - high.astype(jnp.float32)).astype(jnp.bfloat16)
    return high, low


def nt_dot(a, b):
    return lax.dot_general(a, b, (((1,), (1,)), ((), ())), preferred_element_type=jnp.float32)


def tn_dot(a, b):
    return lax.dot_general(a, b, (((0,), (0,)), ((), ())), preferred_element_type=jnp.float32)


def iota(shape, axis):
    return lax.broadcasted_iota(jnp.int32, shape, axis)


def kernel(
    n, nb, page_rows, w_chunks,
    own_ref, tab_ref, len_ref, k_ref, v_ref, ck_ref, cv_ref, dq_ref, dk_ref, dv_ref, q_hbm, w_hbm,
    out_ref, dec_ref,
    kv, q_vm, w_vm, page_send, page_recv, count_send, count_recv, acc_all, stat_all,
    q8, dk8, dv8, y_send, y_recv,
    local_sem, ring_send, ring_recv, page_ss, page_rs, count_ss, count_rs,
    acc_ss, acc_rs, stat_ss, stat_rs, y_ss, y_rs,
):
    me = lax.axis_index("seq")
    mb = lax.axis_index("batch")
    mt = lax.axis_index("tp")
    tok = k_ref.shape[1]
    kw = k_ref.shape[2]
    k_heads = kw // HD
    q_heads = q_vm.shape[1] // HD
    group = q_heads // k_heads
    new, requests, _ = dq_ref.shape
    pages = tok // page_rows
    slots = tab_ref.shape[1]
    pool = ck_ref.shape[0]
    scaling = HD ** (-0.5)
    other = 1 - mt

    q_copy = pltpu.make_async_copy(q_hbm.at[0], q_vm, local_sem.at[0])
    w_copy = pltpu.make_async_copy(w_hbm, w_vm, local_sem.at[1])
    q_copy.start()
    w_copy.start()

    barrier = pltpu.get_barrier_semaphore()
    for k in range(1, n):
        pl.semaphore_signal(barrier, inc=1, device_id={"seq": lax.rem(me + k, n)}, device_id_type=pl.DeviceIdType.MESH)
    for k in range(1, nb):
        pl.semaphore_signal(barrier, inc=1, device_id={"batch": lax.rem(mb + k, nb)}, device_id_type=pl.DeviceIdType.MESH)
    pl.semaphore_signal(barrier, inc=1, device_id={"tp": other}, device_id_type=pl.DeviceIdType.MESH)

    kv[me, :, 0:kw] = k_ref[0]
    kv[me, :, kw:2 * kw] = v_ref[0]

    owners = [own_ref[0, 0, j] for j in range(pages)]
    ranks = []
    for j in range(pages):
        rank = jnp.int32(0)
        for i in range(j):
            rank = rank + jnp.where(owners[i] == owners[j], 1, 0)
        ranks.append(rank)
    wide = MOST * page_rows
    source_page = iota((1, tok), 1) // page_rows
    place = jnp.zeros((1, tok), jnp.int32)
    for j in range(pages):
        place = jnp.where(source_page == j, owners[j] * MOST + ranks[j], place)
    row = iota((nb * wide, tok), 0)
    column = iota((nb * wide, tok), 1)
    chosen = (row // page_rows == place) & (row % page_rows == column % page_rows)
    chosen = jnp.where(chosen, 1.0, 0.0).astype(jnp.bfloat16)
    for half, ref in enumerate((k_ref, v_ref)):
        moved = jnp.dot(chosen, ref[0], preferred_element_type=jnp.float32)
        page_send[:, :, half * kw:(half + 1) * kw] = moved.astype(jnp.bfloat16).reshape(nb, wide, kw)
    for o in range(nb):
        count = jnp.int32(0)
        for j in range(pages):
            count = count + jnp.where(owners[j] == o, 1, 0)
        count_send[o] = jnp.full((ROWS, LANES), count, jnp.int32)
    page_recv[mb] = page_send[mb]
    count_recv[mb] = count_send[mb]

    pl.semaphore_wait(barrier, (n - 1) + (nb - 1) + 1)

    def ring(i):
        block = me - i
        return pltpu.make_async_remote_copy(
            src_ref=kv.at[block], dst_ref=kv.at[block], send_sem=ring_send.at[i], recv_sem=ring_recv.at[i],
            device_id={"seq": me + 1}, device_id_type=pl.DeviceIdType.MESH)

    def arrival(i):
        block = me - 1 - i
        return pltpu.make_async_remote_copy(
            src_ref=kv.at[block], dst_ref=kv.at[block], send_sem=ring_send.at[i], recv_sem=ring_recv.at[i],
            device_id={"seq": me - 1}, device_id_type=pl.DeviceIdType.MESH)

    def page_pair(k):
        to = lax.rem(mb + k, nb)
        return (
            pltpu.make_async_remote_copy(
                src_ref=count_send.at[to], dst_ref=count_recv.at[mb], send_sem=count_ss.at[k - 1],
                recv_sem=count_rs.at[k - 1], device_id={"batch": to}, device_id_type=pl.DeviceIdType.MESH),
            pltpu.make_async_remote_copy(
                src_ref=page_send.at[to], dst_ref=page_recv.at[mb], send_sem=page_ss.at[k - 1],
                recv_sem=page_rs.at[k - 1], device_id={"batch": to}, device_id_type=pl.DeviceIdType.MESH),
        )

    def page_arrival(k):
        since = lax.rem(mb - k + nb, nb)
        return (
            pltpu.make_async_remote_copy(
                src_ref=count_send.at[since], dst_ref=count_recv.at[since], send_sem=count_ss.at[k - 1],
                recv_sem=count_rs.at[k - 1], device_id={"batch": since}, device_id_type=pl.DeviceIdType.MESH),
            pltpu.make_async_remote_copy(
                src_ref=page_send.at[since], dst_ref=page_recv.at[since], send_sem=page_ss.at[k - 1],
                recv_sem=page_rs.at[k - 1], device_id={"batch": since}, device_id_type=pl.DeviceIdType.MESH),
        )

    @pl.when(me < n - 1)
    def _():
        ring(0).start()

    for k in range(1, nb):
        for copy in page_pair(k):
            copy.start()

    def relay(i):
        @pl.when(me > i)
        def _():
            arrival(i).wait_recv()

            @pl.when(me < n - 1)
            def _():
                ring(i + 1).start()

    for j in range(1, n):
        @pl.when(j > me)
        def _():
            kv[j] = jnp.zeros_like(kv[j])

    for packed, ref in ((q8, dq_ref), (dk8, dk_ref), (dv8, dv_ref)):
        packed[...] = jnp.zeros_like(packed)
        for m in range(new):
            packed[m * requests:(m + 1) * requests, :] = ref[m]
    per_head = group * ROWS
    diagonal = []
    for a in range(k_heads):
        rows = jnp.concatenate(
            [q8[:, (a * group + g) * HD:(a * group + g + 1) * HD] for g in range(group)], axis=0)
        nothing = jnp.zeros((per_head, HD), jnp.float32)
        diagonal.append(jnp.concatenate([rows if b == a else nothing for b in range(k_heads)], axis=1))
    dec_q = jnp.concatenate(halves(jnp.concatenate(diagonal, axis=0)), axis=0)
    lanes = k_heads * per_head

    def dec_scores(keys):
        both = nt_dot(keys, dec_q)
        return (both[:, :lanes] + both[:, lanes:]) * scaling

    cache_rows = pool * page_rows
    token = iota((1, lanes), 1) % ROWS
    request = token % requests
    score_cache = dec_scores(ck_ref[...].reshape(cache_rows, kw))
    slot_of = iota((cache_rows, lanes), 0) // page_rows
    within = iota((cache_rows, lanes), 0) % page_rows
    live = jnp.zeros((cache_rows, lanes), jnp.int32)
    for r in range(requests):
        for j in range(slots):
            first = (j * n + me) * page_rows
            named = (slot_of == tab_ref[r, j]) & (request == r) & (first + within < len_ref[r])
            live = jnp.where(named, 1, live)
    score_cache = jnp.where(live > 0, score_cache, floor_score)
    new_k = jnp.concatenate([part.astype(jnp.float32) for part in halves(dk8[...])], axis=0).astype(jnp.bfloat16)
    new_v = jnp.concatenate([part.astype(jnp.float32) for part in halves(dv8[...])], axis=0).astype(jnp.bfloat16)
    score_new = dec_scores(new_k)
    score_new = score_new[:ROWS] + score_new[ROWS:]
    key_token = iota((ROWS, lanes), 0)
    causal = (key_token % requests == request) & (key_token <= token) & (me == 0)
    score_new = jnp.where(causal, score_new, floor_score)

    relay(0)

    for k in range(1, nb):
        for copy in page_arrival(k):
            copy.wait_recv()
    received = page_recv[...].reshape(nb * wide, 2 * kw)
    score_recv = dec_scores(received[:, :kw])
    place_of = iota((wide, lanes), 0) // page_rows
    kept = jnp.concatenate([jnp.where(place_of < count_recv[b][0:1, :], 1, 0) for b in range(nb)], axis=0)
    score_recv = jnp.where(kept > 0, score_recv, floor_score)
    peak = jnp.maximum(
        jnp.maximum(jnp.max(score_cache, axis=0, keepdims=True), jnp.max(score_recv, axis=0, keepdims=True)),
        jnp.max(score_new, axis=0, keepdims=True))
    weight_cache = jnp.where(live > 0, jnp.exp(score_cache - peak), 0.0)
    weight_recv = jnp.where(kept > 0, jnp.exp(score_recv - peak), 0.0)
    weight_new = jnp.where(causal, jnp.exp(score_new - peak), 0.0)
    total = (jnp.sum(weight_cache, axis=0, keepdims=True) + jnp.sum(weight_recv, axis=0, keepdims=True)
             + jnp.sum(weight_new, axis=0, keepdims=True))

    def dec_values(values, weights):
        both = tn_dot(values, jnp.concatenate(halves(weights), axis=1))
        return both[:, :lanes] + both[:, lanes:]

    mixed = dec_values(cv_ref[...].reshape(cache_rows, kw), weight_cache)
    mixed = mixed + dec_values(received[:, kw:], weight_recv)
    mixed = mixed + dec_values(new_v, jnp.concatenate([weight_new, weight_new], axis=0))
    lane_head = iota((HD, lanes), 1) // per_head
    acc = mixed[0:HD]
    for a in range(1, k_heads):
        acc = jnp.where(lane_head == a, mixed[a * HD:(a + 1) * HD], acc)
    acc_all[me] = acc.astype(jnp.bfloat16)
    stat_row = iota((ROWS, lanes), 0)
    stat_all[me] = jnp.where(stat_row == 0, peak, total)

    def partial_pair(k, slot, to):
        return (
            pltpu.make_async_remote_copy(
                src_ref=acc_all.at[slot], dst_ref=acc_all.at[slot], send_sem=acc_ss.at[k - 1],
                recv_sem=acc_rs.at[k - 1], device_id={"seq": to}, device_id_type=pl.DeviceIdType.MESH),
            pltpu.make_async_remote_copy(
                src_ref=stat_all.at[slot], dst_ref=stat_all.at[slot], send_sem=stat_ss.at[k - 1],
                recv_sem=stat_rs.at[k - 1], device_id={"seq": to}, device_id_type=pl.DeviceIdType.MESH),
        )

    for k in range(1, n):
        for copy in partial_pair(k, me, lax.rem(me + k, n)):
            copy.start()

    for i in range(1, n - 2):
        relay(i)

    for k in range(1, n):
        since = lax.rem(me - k + n, n)
        for copy in partial_pair(k, since, since):
            copy.wait_recv()
    peaks = [stat_all[s][0:1, :] for s in range(n)]
    top = functools.reduce(jnp.maximum, peaks)
    scales = [jnp.exp(p - top) for p in peaks]
    whole = sum(stat_all[s][1:2, :] * scales[s] for s in range(n))
    merged = sum(acc_all[s].astype(jnp.float32) * scales[s] for s in range(n)) / whole
    merged = merged.T
    attention = jnp.concatenate([merged[h * ROWS:(h + 1) * ROWS] for h in range(q_heads)], axis=1)
    parts = jnp.concatenate([p.astype(jnp.float32) for p in halves(attention)], axis=0).astype(jnp.bfloat16)
    w_copy.wait()
    step = w_vm.shape[1] // w_chunks

    def y_copy(c):
        return pltpu.make_async_remote_copy(
            src_ref=y_send.at[c], dst_ref=y_recv.at[c], send_sem=y_ss.at[c], recv_sem=y_rs.at[c],
            device_id={"tp": other}, device_id_type=pl.DeviceIdType.MESH)

    for c in range(w_chunks):
        both = jnp.dot(parts, w_vm[:, c * step:(c + 1) * step], preferred_element_type=jnp.float32)
        y_send[c] = both[:ROWS] + both[ROWS:]
        y_copy(c).start()

    q_copy.wait()

    @pl.when(me > n - 2)
    def _():
        arrival(n - 2).wait_recv()

    visible = iota((tok, n * tok), 1) <= iota((tok, n * tok), 0) + me * tok
    at_once = min(4, group)
    for a in range(k_heads):
        def heads(step_id, carry, a=a):
            keys = kv[:, :, a * HD:(a + 1) * HD].reshape(n * tok, HD)
            values = kv[:, :, kw + a * HD:kw + (a + 1) * HD].reshape(n * tok, HD)
            for g in range(at_once):
                start = pl.multiple_of((a * group + step_id * at_once + g) * HD, HD)
                scores = nt_dot(q_vm[:, pl.ds(start, HD)], keys) * scaling
                scores = jnp.where(visible, scores, floor_score)
                weights = jnp.exp(scores - jnp.max(scores, axis=1, keepdims=True))
                sums = jnp.sum(weights, axis=1, keepdims=True)
                mixture = jnp.dot(weights.astype(jnp.bfloat16), values, preferred_element_type=jnp.float32)
                out_ref[0, :, pl.ds(start, HD)] = (mixture / sums).astype(jnp.bfloat16)
            return carry

        lax.fori_loop(0, group // at_once, heads, 0)

    for c in range(w_chunks):
        y_copy(c).wait()
        y = y_send[c] + y_recv[c]
        for m in range(new):
            dec_ref[m, :, c * step:(c + 1) * step] = y[m * requests:(m + 1) * requests]

    for i in range(n - 1):
        @pl.when((me < n - 1) & (me >= i))
        def _():
            ring(i).wait_send()
    for k in range(1, nb):
        for copy in page_pair(k):
            copy.wait_send()
    for k in range(1, n):
        for copy in partial_pair(k, me, lax.rem(me + k, n)):
            copy.wait_send()


def local(
    pre_q, pre_k, pre_v, owner_map, cache_k, cache_v, tables, lengths, dec_q, dec_k, dec_v, w_out
):
    n = lax.axis_size("seq")
    nb = lax.axis_size("batch")
    tok = pre_q.shape[1]
    kw = pre_k.shape[2]
    page_rows = cache_k.shape[1]
    lanes = pre_q.shape[2] // HD * ROWS
    out_columns = w_out.shape[1]
    w_chunks = max(1, out_columns // 512)
    smem = pl.BlockSpec(memory_space=pltpu.SMEM)
    vmem = pl.BlockSpec(memory_space=pltpu.VMEM)
    anywhere = pl.BlockSpec(memory_space=pl.ANY)
    dma = pltpu.SemaphoreType.DMA
    pre_out, dec_out = pl.pallas_call(
        functools.partial(kernel, n, nb, page_rows, w_chunks),
        out_shape=(
            jax.ShapeDtypeStruct(pre_q.shape, jnp.bfloat16),
            jax.ShapeDtypeStruct((dec_q.shape[1], dec_q.shape[0], out_columns), jnp.float32),
        ),
        in_specs=[smem] * 3 + [vmem] * 7 + [anywhere] * 2,
        out_specs=(vmem, vmem),
        scratch_shapes=[
            pltpu.VMEM((n, tok, 2 * kw), jnp.bfloat16),
            pltpu.VMEM((tok, pre_q.shape[2]), jnp.bfloat16),
            pltpu.VMEM(w_out.shape, jnp.bfloat16),
            pltpu.VMEM((nb, MOST * page_rows, 2 * kw), jnp.bfloat16),
            pltpu.VMEM((nb, MOST * page_rows, 2 * kw), jnp.bfloat16),
            pltpu.VMEM((nb, ROWS, LANES), jnp.int32),
            pltpu.VMEM((nb, ROWS, LANES), jnp.int32),
            pltpu.VMEM((n, HD, lanes), jnp.bfloat16),
            pltpu.VMEM((n, ROWS, lanes), jnp.float32),
            pltpu.VMEM((ROWS, dec_q.shape[2]), jnp.float32),
            pltpu.VMEM((ROWS, kw), jnp.float32),
            pltpu.VMEM((ROWS, kw), jnp.float32),
            pltpu.VMEM((w_chunks, ROWS, out_columns // w_chunks), jnp.float32),
            pltpu.VMEM((w_chunks, ROWS, out_columns // w_chunks), jnp.float32),
            dma((2,)),
            dma((n - 1,)), dma((n - 1,)),
            dma((nb - 1,)), dma((nb - 1,)), dma((nb - 1,)), dma((nb - 1,)),
            dma((n - 1,)), dma((n - 1,)), dma((n - 1,)), dma((n - 1,)),
            dma((w_chunks,)), dma((w_chunks,)),
        ],
        compiler_params=pltpu.CompilerParams(
            collective_id=0, has_side_effects=True, vmem_limit_bytes=48 * 1024 * 1024
        ),
        name="prefill_and_decode",
    )(
        jnp.swapaxes(owner_map, 1, 2), tables, lengths, pre_k, pre_v, cache_k, cache_v,
        *(jnp.swapaxes(x, 0, 1) for x in (dec_q, dec_k, dec_v)), pre_q, w_out,
    )
    return pre_out, jnp.swapaxes(dec_out, 0, 1)


def solution(mesh):
    placed = (
        P("batch", "seq", "tp"),
        P("batch", "seq", "tp"),
        P("batch", "seq", "tp"),
        P("batch", "seq", None),
        P("batch", "seq", "tp"),
        P("batch", "seq", "tp"),
        P("batch", "seq"),
        P("batch"),
        P("batch", None, "tp"),
        P("batch", None, "tp"),
        P("batch", None, "tp"),
        P("tp", "seq"),
    )
    return jax.shard_map(
        local,
        mesh=mesh,
        in_specs=placed,
        out_specs=(P("batch", "seq", "tp"), P("batch", None, "seq")),
        check_vma=False,
    )
```

```python
import functools

import jax
import jax.numpy as jnp
from jax import lax
from jax.experimental import pallas as pl
from jax.experimental.pallas import tpu as pltpu
from jax.sharding import PartitionSpec as P

HD = 128
MOST = 4
ROWS = 8
LANES = 128
floor_score = -1e30


def halves(x):
    high = x.astype(jnp.bfloat16)
    low = (x - high.astype(jnp.float32)).astype(jnp.bfloat16)
    return high, low


def nt_dot(a, b):
    return lax.dot_general(a, b, (((1,), (1,)), ((), ())), preferred_element_type=jnp.float32)


def tn_dot(a, b):
    return lax.dot_general(a, b, (((0,), (0,)), ((), ())), preferred_element_type=jnp.float32)


def iota(shape, axis):
    return lax.broadcasted_iota(jnp.int32, shape, axis)


def kernel(
    n, nb, page_rows, w_chunks,
    own_hbm, tab_hbm, len_hbm, k_hbm, v_hbm, ck_hbm, cv_hbm, dq_hbm, dk_hbm, dv_hbm, q_hbm, w_hbm,
    out_hbm, dec_ref,
    out_ref, own_ref, tab_ref, len_ref, ck_ref, cv_ref, dq_ref, dk_ref, dv_ref, mix_ref, peak_ref, total_ref,
    kv, q_vm, w_vm, page_send, page_recv, count_send, count_recv, acc_all, stat_all,
    q8, dk8, dv8, y_send, y_recv,
    local_sem, out_sem, ring_send, ring_recv, page_ss, page_rs, count_ss, count_rs,
    acc_ss, acc_rs, stat_ss, stat_rs, y_ss, y_rs,
):
    me = lax.axis_index("seq")
    mb = lax.axis_index("batch")
    mt = lax.axis_index("tp")
    tok = k_hbm.shape[1]
    kw = k_hbm.shape[2]
    k_heads = kw // HD
    q_heads = q_vm.shape[1] // HD
    group = q_heads // k_heads
    new, requests, _ = dq_ref.shape
    pages = tok // page_rows
    slots = tab_ref.shape[1]
    pool = ck_ref.shape[0]
    scaling = HD ** (-0.5)
    other = 1 - mt

    barrier = pltpu.get_barrier_semaphore()
    for k in range(1, n):
        pl.semaphore_signal(barrier, inc=1, device_id={"seq": lax.rem(me + k, n)}, device_id_type=pl.DeviceIdType.MESH)
    for k in range(1, nb):
        pl.semaphore_signal(barrier, inc=1, device_id={"batch": lax.rem(mb + k, nb)}, device_id_type=pl.DeviceIdType.MESH)
    pl.semaphore_signal(barrier, inc=1, device_id={"tp": other}, device_id_type=pl.DeviceIdType.MESH)

    mine = kv.at[me]
    sources = (
        (k_hbm.at[0], mine.at[:, pl.ds(0, kw)]), (v_hbm.at[0], mine.at[:, pl.ds(kw, kw)]), (own_hbm, own_ref),
        (dq_hbm, dq_ref), (dk_hbm, dk_ref), (dv_hbm, dv_ref), (tab_hbm, tab_ref), (len_hbm, len_ref),
        (ck_hbm, ck_ref), (cv_hbm, cv_ref), (q_hbm.at[0], q_vm), (w_hbm, w_vm))
    copies = [pltpu.make_async_copy(a, b, local_sem.at[i]) for i, (a, b) in enumerate(sources)]
    for copy in copies:
        copy.start()
    w_copy = copies.pop()
    q_copy = copies.pop()
    for copy in copies[:3]:
        copy.wait()

    owners = [own_ref[0, 0, j] for j in range(pages)]
    ranks = []
    for j in range(pages):
        rank = jnp.int32(0)
        for i in range(j):
            rank = rank + jnp.where(owners[i] == owners[j], 1, 0)
        ranks.append(rank)
    wide = MOST * page_rows
    source_page = iota((1, tok), 1) // page_rows
    place = jnp.zeros((1, tok), jnp.int32)
    for j in range(pages):
        place = jnp.where(source_page == j, owners[j] * MOST + ranks[j], place)
    row = iota((nb * wide, tok), 0)
    column = iota((nb * wide, tok), 1)
    chosen = (row // page_rows == place) & (row % page_rows == column % page_rows)
    chosen = jnp.where(chosen, 1.0, 0.0).astype(jnp.bfloat16)
    moved = jnp.dot(chosen, kv[me], preferred_element_type=jnp.float32)
    page_send[...] = moved.astype(jnp.bfloat16).reshape(nb, wide, 2 * kw)
    for o in range(nb):
        count = jnp.int32(0)
        for j in range(pages):
            count = count + jnp.where(owners[j] == o, 1, 0)
        count_send[o] = jnp.full((ROWS, LANES), count, jnp.int32)
    page_recv[mb] = page_send[mb]
    count_recv[mb] = count_send[mb]

    pl.semaphore_wait(barrier, (n - 1) + (nb - 1) + 1)

    def ring(i):
        block = me - i
        return pltpu.make_async_remote_copy(
            src_ref=kv.at[block], dst_ref=kv.at[block], send_sem=ring_send.at[i], recv_sem=ring_recv.at[i],
            device_id={"seq": me + 1}, device_id_type=pl.DeviceIdType.MESH)

    def arrival(i):
        block = me - 1 - i
        return pltpu.make_async_remote_copy(
            src_ref=kv.at[block], dst_ref=kv.at[block], send_sem=ring_send.at[i], recv_sem=ring_recv.at[i],
            device_id={"seq": me - 1}, device_id_type=pl.DeviceIdType.MESH)

    def page_pair(k):
        to = lax.rem(mb + k, nb)
        return (
            pltpu.make_async_remote_copy(
                src_ref=count_send.at[to], dst_ref=count_recv.at[mb], send_sem=count_ss.at[k - 1],
                recv_sem=count_rs.at[k - 1], device_id={"batch": to}, device_id_type=pl.DeviceIdType.MESH),
            pltpu.make_async_remote_copy(
                src_ref=page_send.at[to], dst_ref=page_recv.at[mb], send_sem=page_ss.at[k - 1],
                recv_sem=page_rs.at[k - 1], device_id={"batch": to}, device_id_type=pl.DeviceIdType.MESH),
        )

    def page_arrival(k):
        since = lax.rem(mb - k + nb, nb)
        return (
            pltpu.make_async_remote_copy(
                src_ref=count_send.at[since], dst_ref=count_recv.at[since], send_sem=count_ss.at[k - 1],
                recv_sem=count_rs.at[k - 1], device_id={"batch": since}, device_id_type=pl.DeviceIdType.MESH),
            pltpu.make_async_remote_copy(
                src_ref=page_send.at[since], dst_ref=page_recv.at[since], send_sem=page_ss.at[k - 1],
                recv_sem=page_rs.at[k - 1], device_id={"batch": since}, device_id_type=pl.DeviceIdType.MESH),
        )

    @pl.when(me < n - 1)
    def _():
        ring(0).start()

    for k in range(1, nb):
        for copy in page_pair(k):
            copy.start()

    def relay(i):
        @pl.when(me > i)
        def _():
            arrival(i).wait_recv()

            @pl.when(me < n - 1)
            def _():
                ring(i + 1).start()

    for copy in copies[3:]:
        copy.wait()

    for packed, ref in ((q8, dq_ref), (dk8, dk_ref), (dv8, dv_ref)):
        packed[...] = jnp.zeros_like(packed)
        for m in range(new):
            packed[m * requests:(m + 1) * requests, :] = ref[m]
    per_head = group * ROWS
    diagonal = []
    for a in range(k_heads):
        rows = jnp.concatenate(
            [q8[:, (a * group + g) * HD:(a * group + g + 1) * HD] for g in range(group)], axis=0)
        nothing = jnp.zeros((per_head, HD), jnp.float32)
        diagonal.append(jnp.concatenate([rows if b == a else nothing for b in range(k_heads)], axis=1))
    dec_q = jnp.concatenate(halves(jnp.concatenate(diagonal, axis=0)), axis=0)
    lanes = k_heads * per_head

    def dec_scores(keys):
        both = nt_dot(keys, dec_q)
        return (both[:, :lanes] + both[:, lanes:]) * scaling

    cache_rows = pool * page_rows
    token = iota((1, lanes), 1) % ROWS
    request = token % requests
    score_cache = dec_scores(ck_ref[...].reshape(cache_rows, kw))
    slot_of = iota((cache_rows, lanes), 0) // page_rows
    within = iota((cache_rows, lanes), 0) % page_rows
    live = jnp.zeros((cache_rows, lanes), jnp.int32)
    for r in range(requests):
        for j in range(slots):
            first = (j * n + me) * page_rows
            named = (slot_of == tab_ref[r, j]) & (request == r) & (first + within < len_ref[r])
            live = jnp.where(named, 1, live)
    score_cache = jnp.where(live > 0, score_cache, floor_score)
    new_k = jnp.concatenate([part.astype(jnp.float32) for part in halves(dk8[...])], axis=0).astype(jnp.bfloat16)
    new_v = jnp.concatenate([part.astype(jnp.float32) for part in halves(dv8[...])], axis=0).astype(jnp.bfloat16)
    score_new = dec_scores(new_k)
    score_new = score_new[:ROWS] + score_new[ROWS:]
    key_token = iota((ROWS, lanes), 0)
    causal = (key_token % requests == request) & (key_token <= token) & (me == 0)
    score_new = jnp.where(causal, score_new, floor_score)

    pair = 2
    pair_lanes = pair * tok

    def prefill_block(block, first):
        for a in range(k_heads):
            keys = kv[block, :, a * HD:(a + 1) * HD]
            values = kv[block, :, kw + a * HD:kw + (a + 1) * HD].T
            for p in range(group // pair):
                at = a * (group // pair) + p
                queries = jnp.concatenate(
                    [q_vm[:, (at * pair + i) * HD:(at * pair + i + 1) * HD] for i in range(pair)], axis=0)
                scores = nt_dot(keys, queries) * scaling
                if first:
                    visible = iota((tok, pair_lanes), 0) <= iota((tok, pair_lanes), 1) % tok
                    scores = jnp.where(visible, scores, floor_score)
                high = jnp.max(scores, axis=0, keepdims=True)
                if not first:
                    before = peak_ref[at, 0:1, :]
                    high = jnp.maximum(high, before)
                weights = jnp.exp(scores - high)
                sums = jnp.sum(weights, axis=0, keepdims=True)
                mixture = jnp.dot(values, weights.astype(jnp.bfloat16), preferred_element_type=jnp.float32)
                if not first:
                    shrink = jnp.exp(before - high)
                    sums = sums + total_ref[at, 0:1, :] * shrink
                    mixture = mixture + mix_ref[at] * shrink
                peak_ref[at, 0:1, :] = high
                total_ref[at, 0:1, :] = sums
                mix_ref[at] = mixture

    q_copy.wait()
    prefill_block(me, True)
    relay(0)

    for k in range(1, nb):
        for copy in page_arrival(k):
            copy.wait_recv()
    received = page_recv[...].reshape(nb * wide, 2 * kw)
    score_recv = dec_scores(received[:, :kw])
    place_of = iota((wide, lanes), 0) // page_rows
    kept = jnp.concatenate([jnp.where(place_of < count_recv[b][0:1, :], 1, 0) for b in range(nb)], axis=0)
    score_recv = jnp.where(kept > 0, score_recv, floor_score)
    peak = jnp.maximum(
        jnp.maximum(jnp.max(score_cache, axis=0, keepdims=True), jnp.max(score_recv, axis=0, keepdims=True)),
        jnp.max(score_new, axis=0, keepdims=True))
    weight_cache = jnp.where(live > 0, jnp.exp(score_cache - peak), 0.0)
    weight_recv = jnp.where(kept > 0, jnp.exp(score_recv - peak), 0.0)
    weight_new = jnp.where(causal, jnp.exp(score_new - peak), 0.0)
    total = (jnp.sum(weight_cache, axis=0, keepdims=True) + jnp.sum(weight_recv, axis=0, keepdims=True)
             + jnp.sum(weight_new, axis=0, keepdims=True))

    def dec_values(values, weights):
        both = tn_dot(values, jnp.concatenate(halves(weights), axis=1))
        return both[:, :lanes] + both[:, lanes:]

    mixed = dec_values(cv_ref[...].reshape(cache_rows, kw), weight_cache)
    mixed = mixed + dec_values(received[:, kw:], weight_recv)
    mixed = mixed + dec_values(new_v, jnp.concatenate([weight_new, weight_new], axis=0))
    lane_head = iota((HD, lanes), 1) // per_head
    acc = mixed[0:HD]
    for a in range(1, k_heads):
        acc = jnp.where(lane_head == a, mixed[a * HD:(a + 1) * HD], acc)
    acc_all[me] = acc.astype(jnp.bfloat16)
    stat_row = iota((ROWS, lanes), 0)
    stat_all[me] = jnp.where(stat_row == 0, peak, total)

    def partial_pair(k, slot, to):
        return (
            pltpu.make_async_remote_copy(
                src_ref=acc_all.at[slot], dst_ref=acc_all.at[slot], send_sem=acc_ss.at[k - 1],
                recv_sem=acc_rs.at[k - 1], device_id={"seq": to}, device_id_type=pl.DeviceIdType.MESH),
            pltpu.make_async_remote_copy(
                src_ref=stat_all.at[slot], dst_ref=stat_all.at[slot], send_sem=stat_ss.at[k - 1],
                recv_sem=stat_rs.at[k - 1], device_id={"seq": to}, device_id_type=pl.DeviceIdType.MESH),
        )

    for k in range(1, n):
        for copy in partial_pair(k, me, lax.rem(me + k, n)):
            copy.start()

    @pl.when(me >= 1)
    def _():
        prefill_block(me - 1, False)

    for k in range(1, n):
        since = lax.rem(me - k + n, n)
        for copy in partial_pair(k, since, since):
            copy.wait_recv()
    peaks = [stat_all[s][0:1, :] for s in range(n)]
    top = functools.reduce(jnp.maximum, peaks)
    scales = [jnp.exp(p - top) for p in peaks]
    whole = sum(stat_all[s][1:2, :] * scales[s] for s in range(n))
    merged = sum(acc_all[s].astype(jnp.float32) * scales[s] for s in range(n)) / whole
    merged = merged.T
    attention = jnp.concatenate([merged[h * ROWS:(h + 1) * ROWS] for h in range(q_heads)], axis=1)
    parts = jnp.concatenate([p.astype(jnp.float32) for p in halves(attention)], axis=0).astype(jnp.bfloat16)
    w_copy.wait()
    step = w_vm.shape[1] // w_chunks

    def y_copy(c):
        return pltpu.make_async_remote_copy(
            src_ref=y_send.at[c], dst_ref=y_recv.at[c], send_sem=y_ss.at[c], recv_sem=y_rs.at[c],
            device_id={"tp": other}, device_id_type=pl.DeviceIdType.MESH)

    for c in range(w_chunks):
        both = jnp.dot(parts, w_vm[:, c * step:(c + 1) * step], preferred_element_type=jnp.float32)
        y_send[c] = both[:ROWS] + both[ROWS:]
        y_copy(c).start()

    def later(i, carry):
        @pl.when(me >= i)
        def _():
            arrival(i - 1).wait_recv()

            @pl.when(me < n - 1)
            def _():
                ring(i).start()

            prefill_block(me - i, False)
        return carry

    lax.fori_loop(2, n, later, 0)

    def out_copy(at):
        columns = pl.ds(at * pair * HD, pair * HD)
        return pltpu.make_async_copy(out_ref.at[:, columns], out_hbm.at[0, :, columns], out_sem.at[at])

    unit = jnp.where(iota((tok, tok), 0) == iota((tok, tok), 1), 1.0, 0.0).astype(jnp.bfloat16)
    for at in range(q_heads // pair):
        done = (mix_ref[at] / total_ref[at, 0:1, :]).astype(jnp.bfloat16)
        for i in range(pair):
            turned = nt_dot(unit, done[:, i * tok:(i + 1) * tok])
            head = at * pair + i
            out_ref[:, head * HD:(head + 1) * HD] = turned.astype(jnp.bfloat16)
        out_copy(at).start()

    for c in range(w_chunks):
        y_copy(c).wait()
        y = y_send[c] + y_recv[c]
        for m in range(new):
            dec_ref[m, :, c * step:(c + 1) * step] = y[m * requests:(m + 1) * requests]

    for at in range(q_heads // pair):
        out_copy(at).wait()
    for i in range(n - 1):
        @pl.when((me < n - 1) & (me >= i))
        def _():
            ring(i).wait_send()
    for k in range(1, nb):
        for copy in page_pair(k):
            copy.wait_send()
    for k in range(1, n):
        for copy in partial_pair(k, me, lax.rem(me + k, n)):
            copy.wait_send()


def local(
    pre_q, pre_k, pre_v, owner_map, cache_k, cache_v, tables, lengths, dec_q, dec_k, dec_v, w_out
):
    n = lax.axis_size("seq")
    nb = lax.axis_size("batch")
    tok = pre_q.shape[1]
    kw = pre_k.shape[2]
    page_rows = cache_k.shape[1]
    lanes = pre_q.shape[2] // HD * ROWS
    out_columns = w_out.shape[1]
    w_chunks = max(1, out_columns // 512)
    vmem = pl.BlockSpec(memory_space=pltpu.VMEM)
    hbm = pl.BlockSpec(memory_space=pltpu.HBM)
    dma = pltpu.SemaphoreType.DMA
    pre_out, dec_out = pl.pallas_call(
        functools.partial(kernel, n, nb, page_rows, w_chunks),
        out_shape=(
            jax.ShapeDtypeStruct(pre_q.shape, jnp.bfloat16),
            jax.ShapeDtypeStruct((dec_q.shape[1], dec_q.shape[0], out_columns), jnp.float32),
        ),
        in_specs=[hbm] * 12,
        out_specs=(hbm, vmem),
        scratch_shapes=[
            pltpu.VMEM(pre_q.shape[1:], jnp.bfloat16),
            pltpu.SMEM((1, 1, owner_map.shape[1]), jnp.int32),
            pltpu.SMEM(tables.shape, jnp.int32),
            pltpu.SMEM(lengths.shape, jnp.int32),
            pltpu.VMEM(cache_k.shape, jnp.bfloat16),
            pltpu.VMEM(cache_v.shape, jnp.bfloat16),
            pltpu.VMEM((dec_q.shape[1], dec_q.shape[0], dec_q.shape[2]), jnp.float32),
            pltpu.VMEM((dec_q.shape[1], dec_q.shape[0], kw), jnp.float32),
            pltpu.VMEM((dec_q.shape[1], dec_q.shape[0], kw), jnp.float32),
            pltpu.VMEM((lanes // (2 * ROWS), HD, 2 * tok), jnp.float32),
            pltpu.VMEM((lanes // (2 * ROWS), ROWS, 2 * tok), jnp.float32),
            pltpu.VMEM((lanes // (2 * ROWS), ROWS, 2 * tok), jnp.float32),
            pltpu.VMEM((n, tok, 2 * kw), jnp.bfloat16),
            pltpu.VMEM((tok, pre_q.shape[2]), jnp.bfloat16),
            pltpu.VMEM(w_out.shape, jnp.bfloat16),
            pltpu.VMEM((nb, MOST * page_rows, 2 * kw), jnp.bfloat16),
            pltpu.VMEM((nb, MOST * page_rows, 2 * kw), jnp.bfloat16),
            pltpu.VMEM((nb, ROWS, LANES), jnp.int32),
            pltpu.VMEM((nb, ROWS, LANES), jnp.int32),
            pltpu.VMEM((n, HD, lanes), jnp.bfloat16),
            pltpu.VMEM((n, ROWS, lanes), jnp.float32),
            pltpu.VMEM((ROWS, dec_q.shape[2]), jnp.float32),
            pltpu.VMEM((ROWS, kw), jnp.float32),
            pltpu.VMEM((ROWS, kw), jnp.float32),
            pltpu.VMEM((w_chunks, ROWS, out_columns // w_chunks), jnp.float32),
            pltpu.VMEM((w_chunks, ROWS, out_columns // w_chunks), jnp.float32),
            dma((12,)), dma((lanes // (2 * ROWS),)),
            dma((n - 1,)), dma((n - 1,)),
            dma((nb - 1,)), dma((nb - 1,)), dma((nb - 1,)), dma((nb - 1,)),
            dma((n - 1,)), dma((n - 1,)), dma((n - 1,)), dma((n - 1,)),
            dma((w_chunks,)), dma((w_chunks,)),
        ],
        compiler_params=pltpu.CompilerParams(
            collective_id=0, has_side_effects=True, vmem_limit_bytes=60 * 1024 * 1024
        ),
        name="prefill_and_decode",
    )(
        jnp.swapaxes(owner_map, 1, 2), tables, lengths, pre_k, pre_v, cache_k, cache_v,
        *(jnp.swapaxes(x, 0, 1) for x in (dec_q, dec_k, dec_v)), pre_q, w_out,
    )
    return pre_out, jnp.swapaxes(dec_out, 0, 1)


def solution(mesh):
    placed = (
        P("batch", "seq", "tp"),
        P("batch", "seq", "tp"),
        P("batch", "seq", "tp"),
        P("batch", "seq", None),
        P("batch", "seq", "tp"),
        P("batch", "seq", "tp"),
        P("batch", "seq"),
        P("batch"),
        P("batch", None, "tp"),
        P("batch", None, "tp"),
        P("batch", None, "tp"),
        P("tp", "seq"),
    )
    return jax.shard_map(
        local,
        mesh=mesh,
        in_specs=placed,
        out_specs=(P("batch", "seq", "tp"), P("batch", None, "seq")),
        check_vma=False,
    )
```

```python
import functools

import jax
import jax.numpy as jnp
from jax import lax
from jax.experimental import pallas as pl
from jax.experimental.pallas import tpu as pltpu
from jax.sharding import PartitionSpec as P

HD = 128
MOST = 4
ROWS = 8
LANES = 128
floor_score = -1e30


def halves(x):
    high = x.astype(jnp.bfloat16)
    low = (x - high.astype(jnp.float32)).astype(jnp.bfloat16)
    return high, low


def nt_dot(a, b):
    return lax.dot_general(a, b, (((1,), (1,)), ((), ())), preferred_element_type=jnp.float32)


def tn_dot(a, b):
    return lax.dot_general(a, b, (((0,), (0,)), ((), ())), preferred_element_type=jnp.float32)


def iota(shape, axis):
    return lax.broadcasted_iota(jnp.int32, shape, axis)


def kernel(
    n, nb, page_rows, w_chunks,
    own_hbm, tab_hbm, len_hbm, k_hbm, v_hbm, ck_hbm, cv_hbm, dq_hbm, dk_hbm, dv_hbm, q_hbm, w_hbm,
    out_ref, dec_ref,
    own_ref, tab_ref, len_ref, ck_ref, cv_ref, dq_ref, dk_ref, dv_ref, mix_ref, peak_ref, total_ref,
    kv, q_vm, w_vm, page_send, page_recv, count_send, count_recv, acc_all, stat_all,
    q8, dk8, dv8, y_send, y_recv,
    local_sem, ring_send, ring_recv, page_ss, page_rs, count_ss, count_rs,
    acc_ss, acc_rs, stat_ss, stat_rs, y_ss, y_rs,
):
    me = lax.axis_index("seq")
    mb = lax.axis_index("batch")
    mt = lax.axis_index("tp")
    tok = k_hbm.shape[1]
    kw = k_hbm.shape[2]
    k_heads = kw // HD
    q_heads = q_vm.shape[1] // HD
    group = q_heads // k_heads
    new, requests, _ = dq_ref.shape
    pages = tok // page_rows
    slots = tab_ref.shape[1]
    pool = ck_ref.shape[0]
    scaling = HD ** (-0.5)
    other = 1 - mt

    barrier = pltpu.get_barrier_semaphore()
    for k in range(1, n):
        pl.semaphore_signal(barrier, inc=1, device_id={"seq": lax.rem(me + k, n)}, device_id_type=pl.DeviceIdType.MESH)
    for k in range(1, nb):
        pl.semaphore_signal(barrier, inc=1, device_id={"batch": lax.rem(mb + k, nb)}, device_id_type=pl.DeviceIdType.MESH)
    pl.semaphore_signal(barrier, inc=1, device_id={"tp": other}, device_id_type=pl.DeviceIdType.MESH)

    mine = kv.at[me]
    sources = (
        (k_hbm.at[0], mine.at[:, pl.ds(0, kw)]), (v_hbm.at[0], mine.at[:, pl.ds(kw, kw)]), (own_hbm, own_ref),
        (dq_hbm, dq_ref), (dk_hbm, dk_ref), (dv_hbm, dv_ref), (tab_hbm, tab_ref), (len_hbm, len_ref),
        (ck_hbm, ck_ref), (cv_hbm, cv_ref), (q_hbm.at[0], q_vm), (w_hbm, w_vm))
    copies = [pltpu.make_async_copy(a, b, local_sem.at[i]) for i, (a, b) in enumerate(sources)]
    for copy in copies:
        copy.start()
    w_copy = copies.pop()
    q_copy = copies.pop()
    for copy in copies[:3]:
        copy.wait()

    owners = [own_ref[0, 0, j] for j in range(pages)]
    ranks = []
    for j in range(pages):
        rank = jnp.int32(0)
        for i in range(j):
            rank = rank + jnp.where(owners[i] == owners[j], 1, 0)
        ranks.append(rank)
    wide = MOST * page_rows
    source_page = iota((1, tok), 1) // page_rows
    place = jnp.zeros((1, tok), jnp.int32)
    for j in range(pages):
        place = jnp.where(source_page == j, owners[j] * MOST + ranks[j], place)
    row = iota((nb * wide, tok), 0)
    column = iota((nb * wide, tok), 1)
    chosen = (row // page_rows == place) & (row % page_rows == column % page_rows)
    chosen = jnp.where(chosen, 1.0, 0.0).astype(jnp.bfloat16)
    moved = jnp.dot(chosen, kv[me], preferred_element_type=jnp.float32)
    page_send[...] = moved.astype(jnp.bfloat16).reshape(nb, wide, 2 * kw)
    for o in range(nb):
        count = jnp.int32(0)
        for j in range(pages):
            count = count + jnp.where(owners[j] == o, 1, 0)
        count_send[o] = jnp.full((ROWS, LANES), count, jnp.int32)
    page_recv[mb] = page_send[mb]
    count_recv[mb] = count_send[mb]

    pl.semaphore_wait(barrier, (n - 1) + (nb - 1) + 1)

    def ring(i):
        block = me - i
        return pltpu.make_async_remote_copy(
            src_ref=kv.at[block], dst_ref=kv.at[block], send_sem=ring_send.at[i], recv_sem=ring_recv.at[i],
            device_id={"seq": me + 1}, device_id_type=pl.DeviceIdType.MESH)

    def arrival(i):
        block = me - 1 - i
        return pltpu.make_async_remote_copy(
            src_ref=kv.at[block], dst_ref=kv.at[block], send_sem=ring_send.at[i], recv_sem=ring_recv.at[i],
            device_id={"seq": me - 1}, device_id_type=pl.DeviceIdType.MESH)

    def page_pair(k):
        to = lax.rem(mb + k, nb)
        return (
            pltpu.make_async_remote_copy(
                src_ref=count_send.at[to], dst_ref=count_recv.at[mb], send_sem=count_ss.at[k - 1],
                recv_sem=count_rs.at[k - 1], device_id={"batch": to}, device_id_type=pl.DeviceIdType.MESH),
            pltpu.make_async_remote_copy(
                src_ref=page_send.at[to], dst_ref=page_recv.at[mb], send_sem=page_ss.at[k - 1],
                recv_sem=page_rs.at[k - 1], device_id={"batch": to}, device_id_type=pl.DeviceIdType.MESH),
        )

    def page_arrival(k):
        since = lax.rem(mb - k + nb, nb)
        return (
            pltpu.make_async_remote_copy(
                src_ref=count_send.at[since], dst_ref=count_recv.at[since], send_sem=count_ss.at[k - 1],
                recv_sem=count_rs.at[k - 1], device_id={"batch": since}, device_id_type=pl.DeviceIdType.MESH),
            pltpu.make_async_remote_copy(
                src_ref=page_send.at[since], dst_ref=page_recv.at[since], send_sem=page_ss.at[k - 1],
                recv_sem=page_rs.at[k - 1], device_id={"batch": since}, device_id_type=pl.DeviceIdType.MESH),
        )

    @pl.when(me < n - 1)
    def _():
        ring(0).start()

    for k in range(1, nb):
        for copy in page_pair(k):
            copy.start()

    def relay(i):
        @pl.when(me > i)
        def _():
            arrival(i).wait_recv()

            @pl.when(me < n - 1)
            def _():
                ring(i + 1).start()

    for copy in copies[3:]:
        copy.wait()

    for packed, ref in ((q8, dq_ref), (dk8, dk_ref), (dv8, dv_ref)):
        packed[...] = jnp.zeros_like(packed)
        for m in range(new):
            packed[m * requests:(m + 1) * requests, :] = ref[m]
    per_head = group * ROWS
    diagonal = []
    for a in range(k_heads):
        rows = jnp.concatenate(
            [q8[:, (a * group + g) * HD:(a * group + g + 1) * HD] for g in range(group)], axis=0)
        nothing = jnp.zeros((per_head, HD), jnp.float32)
        diagonal.append(jnp.concatenate([rows if b == a else nothing for b in range(k_heads)], axis=1))
    dec_q = jnp.concatenate(halves(jnp.concatenate(diagonal, axis=0)), axis=0)
    lanes = k_heads * per_head

    def dec_scores(keys):
        both = nt_dot(keys, dec_q)
        return (both[:, :lanes] + both[:, lanes:]) * scaling

    cache_rows = pool * page_rows
    token = iota((1, lanes), 1) % ROWS
    request = token % requests
    score_cache = dec_scores(ck_ref[...].reshape(cache_rows, kw))
    slot_of = iota((cache_rows, lanes), 0) // page_rows
    within = iota((cache_rows, lanes), 0) % page_rows
    live = jnp.zeros((cache_rows, lanes), jnp.int32)
    for r in range(requests):
        for j in range(slots):
            first = (j * n + me) * page_rows
            named = (slot_of == tab_ref[r, j]) & (request == r) & (first + within < len_ref[r])
            live = jnp.where(named, 1, live)
    score_cache = jnp.where(live > 0, score_cache, floor_score)
    new_k = jnp.concatenate([part.astype(jnp.float32) for part in halves(dk8[...])], axis=0).astype(jnp.bfloat16)
    new_v = jnp.concatenate([part.astype(jnp.float32) for part in halves(dv8[...])], axis=0).astype(jnp.bfloat16)
    score_new = dec_scores(new_k)
    score_new = score_new[:ROWS] + score_new[ROWS:]
    key_token = iota((ROWS, lanes), 0)
    causal = (key_token % requests == request) & (key_token <= token) & (me == 0)
    score_new = jnp.where(causal, score_new, floor_score)

    pair = 2
    pair_lanes = pair * tok

    def prefill_block(block, first):
        for a in range(k_heads):
            keys = kv[block, :, a * HD:(a + 1) * HD]
            values = kv[block, :, kw + a * HD:kw + (a + 1) * HD].T
            for p in range(group // pair):
                at = a * (group // pair) + p
                queries = jnp.concatenate(
                    [q_vm[:, (at * pair + i) * HD:(at * pair + i + 1) * HD] for i in range(pair)], axis=0)
                scores = nt_dot(keys, queries) * scaling
                if first:
                    visible = iota((tok, pair_lanes), 0) <= iota((tok, pair_lanes), 1) % tok
                    scores = jnp.where(visible, scores, floor_score)
                high = jnp.max(scores, axis=0, keepdims=True)
                if not first:
                    before = peak_ref[at, 0:1, :]
                    high = jnp.maximum(high, before)
                weights = jnp.exp(scores - high)
                sums = jnp.sum(weights, axis=0, keepdims=True)
                mixture = jnp.dot(values, weights.astype(jnp.bfloat16), preferred_element_type=jnp.float32)
                if not first:
                    shrink = jnp.exp(before - high)
                    sums = sums + total_ref[at, 0:1, :] * shrink
                    mixture = mixture + mix_ref[at] * shrink
                peak_ref[at, 0:1, :] = high
                total_ref[at, 0:1, :] = sums
                mix_ref[at] = mixture

    q_copy.wait()
    prefill_block(me, True)
    relay(0)

    for k in range(1, nb):
        for copy in page_arrival(k):
            copy.wait_recv()
    received = page_recv[...].reshape(nb * wide, 2 * kw)
    score_recv = dec_scores(received[:, :kw])
    place_of = iota((wide, lanes), 0) // page_rows
    kept = jnp.concatenate([jnp.where(place_of < count_recv[b][0:1, :], 1, 0) for b in range(nb)], axis=0)
    score_recv = jnp.where(kept > 0, score_recv, floor_score)
    peak = jnp.maximum(
        jnp.maximum(jnp.max(score_cache, axis=0, keepdims=True), jnp.max(score_recv, axis=0, keepdims=True)),
        jnp.max(score_new, axis=0, keepdims=True))
    weight_cache = jnp.where(live > 0, jnp.exp(score_cache - peak), 0.0)
    weight_recv = jnp.where(kept > 0, jnp.exp(score_recv - peak), 0.0)
    weight_new = jnp.where(causal, jnp.exp(score_new - peak), 0.0)
    total = (jnp.sum(weight_cache, axis=0, keepdims=True) + jnp.sum(weight_recv, axis=0, keepdims=True)
             + jnp.sum(weight_new, axis=0, keepdims=True))

    def dec_values(values, weights):
        both = tn_dot(values, jnp.concatenate(halves(weights), axis=1))
        return both[:, :lanes] + both[:, lanes:]

    mixed = dec_values(cv_ref[...].reshape(cache_rows, kw), weight_cache)
    mixed = mixed + dec_values(received[:, kw:], weight_recv)
    mixed = mixed + dec_values(new_v, jnp.concatenate([weight_new, weight_new], axis=0))
    lane_head = iota((HD, lanes), 1) // per_head
    acc = mixed[0:HD]
    for a in range(1, k_heads):
        acc = jnp.where(lane_head == a, mixed[a * HD:(a + 1) * HD], acc)
    acc_all[me] = acc.astype(jnp.bfloat16)
    stat_row = iota((ROWS, lanes), 0)
    stat_all[me] = jnp.where(stat_row == 0, peak, total)

    def partial_pair(k, slot, to):
        return (
            pltpu.make_async_remote_copy(
                src_ref=acc_all.at[slot], dst_ref=acc_all.at[slot], send_sem=acc_ss.at[k - 1],
                recv_sem=acc_rs.at[k - 1], device_id={"seq": to}, device_id_type=pl.DeviceIdType.MESH),
            pltpu.make_async_remote_copy(
                src_ref=stat_all.at[slot], dst_ref=stat_all.at[slot], send_sem=stat_ss.at[k - 1],
                recv_sem=stat_rs.at[k - 1], device_id={"seq": to}, device_id_type=pl.DeviceIdType.MESH),
        )

    for k in range(1, n):
        for copy in partial_pair(k, me, lax.rem(me + k, n)):
            copy.start()

    @pl.when(me >= 1)
    def _():
        prefill_block(me - 1, False)

    if n > 2:
        relay(1)

    for k in range(1, n):
        since = lax.rem(me - k + n, n)
        for copy in partial_pair(k, since, since):
            copy.wait_recv()
    peaks = [stat_all[s][0:1, :] for s in range(n)]
    top = functools.reduce(jnp.maximum, peaks)
    scales = [jnp.exp(p - top) for p in peaks]
    whole = sum(stat_all[s][1:2, :] * scales[s] for s in range(n))
    merged = sum(acc_all[s].astype(jnp.float32) * scales[s] for s in range(n)) / whole
    merged = merged.T
    attention = jnp.concatenate([merged[h * ROWS:(h + 1) * ROWS] for h in range(q_heads)], axis=1)
    parts = jnp.concatenate([p.astype(jnp.float32) for p in halves(attention)], axis=0).astype(jnp.bfloat16)
    w_copy.wait()
    step = w_vm.shape[1] // w_chunks

    def y_copy(c):
        return pltpu.make_async_remote_copy(
            src_ref=y_send.at[c], dst_ref=y_recv.at[c], send_sem=y_ss.at[c], recv_sem=y_rs.at[c],
            device_id={"tp": other}, device_id_type=pl.DeviceIdType.MESH)

    for c in range(w_chunks):
        both = jnp.dot(parts, w_vm[:, c * step:(c + 1) * step], preferred_element_type=jnp.float32)
        y_send[c] = both[:ROWS] + both[ROWS:]
        y_copy(c).start()

    def later(i, carry):
        @pl.when((me >= i) & (i > 2))
        def _():
            arrival(i - 1).wait_recv()

            @pl.when(me < n - 1)
            def _():
                ring(i).start()

        @pl.when(me >= i)
        def _():
            prefill_block(me - i, False)
        return carry

    lax.fori_loop(2, n, later, 0)

    unit = jnp.where(iota((tok, tok), 0) == iota((tok, tok), 1), 1.0, 0.0).astype(jnp.bfloat16)
    for at in range(q_heads // pair):
        done = (mix_ref[at] / total_ref[at, 0:1, :]).astype(jnp.bfloat16)
        for i in range(pair):
            turned = nt_dot(unit, done[:, i * tok:(i + 1) * tok])
            head = at * pair + i
            out_ref[0, :, head * HD:(head + 1) * HD] = turned.astype(jnp.bfloat16)

    for c in range(w_chunks):
        y_copy(c).wait()
        y = y_send[c] + y_recv[c]
        for m in range(new):
            dec_ref[m, :, c * step:(c + 1) * step] = y[m * requests:(m + 1) * requests]

    for i in range(n - 1):
        @pl.when((me < n - 1) & (me >= i))
        def _():
            ring(i).wait_send()
    for k in range(1, nb):
        for copy in page_pair(k):
            copy.wait_send()
    for k in range(1, n):
        for copy in partial_pair(k, me, lax.rem(me + k, n)):
            copy.wait_send()


def hand_over(pre_ref, dec_ref, pre_hbm, dec_hbm, sems):
    copies = [
        pltpu.make_async_copy(a, b, sems.at[i]) for i, (a, b) in enumerate(((pre_ref, pre_hbm), (dec_ref, dec_hbm)))]
    for copy in copies:
        copy.start()
    for copy in copies:
        copy.wait()


def local(
    pre_q, pre_k, pre_v, owner_map, cache_k, cache_v, tables, lengths, dec_q, dec_k, dec_v, w_out
):
    n = lax.axis_size("seq")
    nb = lax.axis_size("batch")
    tok = pre_q.shape[1]
    kw = pre_k.shape[2]
    page_rows = cache_k.shape[1]
    lanes = pre_q.shape[2] // HD * ROWS
    out_columns = w_out.shape[1]
    w_chunks = max(1, out_columns // 512)
    vmem = pl.BlockSpec(memory_space=pltpu.VMEM)
    hbm = pl.BlockSpec(memory_space=pltpu.HBM)
    dma = pltpu.SemaphoreType.DMA
    pre_out, dec_out = pl.pallas_call(
        functools.partial(kernel, n, nb, page_rows, w_chunks),
        out_shape=(
            pltpu.VMEM(pre_q.shape, jnp.bfloat16),
            pltpu.VMEM((dec_q.shape[1], dec_q.shape[0], out_columns), jnp.float32),
        ),
        in_specs=[hbm] * 12,
        out_specs=(vmem, vmem),
        scratch_shapes=[
            pltpu.SMEM((1, 1, owner_map.shape[1]), jnp.int32),
            pltpu.SMEM(tables.shape, jnp.int32),
            pltpu.SMEM(lengths.shape, jnp.int32),
            pltpu.VMEM(cache_k.shape, jnp.bfloat16),
            pltpu.VMEM(cache_v.shape, jnp.bfloat16),
            pltpu.VMEM((dec_q.shape[1], dec_q.shape[0], dec_q.shape[2]), jnp.float32),
            pltpu.VMEM((dec_q.shape[1], dec_q.shape[0], kw), jnp.float32),
            pltpu.VMEM((dec_q.shape[1], dec_q.shape[0], kw), jnp.float32),
            pltpu.VMEM((lanes // (2 * ROWS), HD, 2 * tok), jnp.float32),
            pltpu.VMEM((lanes // (2 * ROWS), ROWS, 2 * tok), jnp.float32),
            pltpu.VMEM((lanes // (2 * ROWS), ROWS, 2 * tok), jnp.float32),
            pltpu.VMEM((n, tok, 2 * kw), jnp.bfloat16),
            pltpu.VMEM((tok, pre_q.shape[2]), jnp.bfloat16),
            pltpu.VMEM(w_out.shape, jnp.bfloat16),
            pltpu.VMEM((nb, MOST * page_rows, 2 * kw), jnp.bfloat16),
            pltpu.VMEM((nb, MOST * page_rows, 2 * kw), jnp.bfloat16),
            pltpu.VMEM((nb, ROWS, LANES), jnp.int32),
            pltpu.VMEM((nb, ROWS, LANES), jnp.int32),
            pltpu.VMEM((n, HD, lanes), jnp.bfloat16),
            pltpu.VMEM((n, ROWS, lanes), jnp.float32),
            pltpu.VMEM((ROWS, dec_q.shape[2]), jnp.float32),
            pltpu.VMEM((ROWS, kw), jnp.float32),
            pltpu.VMEM((ROWS, kw), jnp.float32),
            pltpu.VMEM((w_chunks, ROWS, out_columns // w_chunks), jnp.float32),
            pltpu.VMEM((w_chunks, ROWS, out_columns // w_chunks), jnp.float32),
            dma((12,)),
            dma((n - 1,)), dma((n - 1,)),
            dma((nb - 1,)), dma((nb - 1,)), dma((nb - 1,)), dma((nb - 1,)),
            dma((n - 1,)), dma((n - 1,)), dma((n - 1,)), dma((n - 1,)),
            dma((w_chunks,)), dma((w_chunks,)),
        ],
        compiler_params=pltpu.CompilerParams(
            collective_id=0, has_side_effects=True, vmem_limit_bytes=48 * 1024 * 1024
        ),
        name="prefill_and_decode",
    )(*(pltpu.with_memory_space_constraint(x, pltpu.HBM) for x in (
        jnp.swapaxes(owner_map, 1, 2), tables, lengths, pre_k, pre_v, cache_k, cache_v,
        *(jnp.swapaxes(x, 0, 1) for x in (dec_q, dec_k, dec_v)), pre_q, w_out,
    )))
    pre_out, dec_out = pl.pallas_call(
        hand_over,
        out_shape=(pltpu.HBM(pre_out.shape, pre_out.dtype), pltpu.HBM(dec_out.shape, dec_out.dtype)),
        in_specs=[vmem] * 2,
        out_specs=(hbm, hbm),
        scratch_shapes=[dma((2,))],
        name="hand_over",
    )(*(pltpu.with_memory_space_constraint(x, pltpu.VMEM) for x in (pre_out, dec_out)))
    return pre_out, jnp.swapaxes(dec_out, 0, 1)


def solution(mesh):
    placed = (
        P("batch", "seq", "tp"),
        P("batch", "seq", "tp"),
        P("batch", "seq", "tp"),
        P("batch", "seq", None),
        P("batch", "seq", "tp"),
        P("batch", "seq", "tp"),
        P("batch", "seq"),
        P("batch"),
        P("batch", None, "tp"),
        P("batch", None, "tp"),
        P("batch", None, "tp"),
        P("tp", "seq"),
    )
    return jax.shard_map(
        local,
        mesh=mesh,
        in_specs=placed,
        out_specs=(P("batch", "seq", "tp"), P("batch", None, "seq")),
        check_vma=False,
    )
```

```python
import functools

import jax
import jax.numpy as jnp
from jax import lax
from jax.experimental import pallas as pl
from jax.experimental.pallas import tpu as pltpu
from jax.sharding import PartitionSpec as P

HD = 128
MOST = 4
ROWS = 8
LANES = 128
floor_score = -1e30
LOG2E = 1.4426950408889634


def halves(x):
    high = x.astype(jnp.bfloat16)
    low = (x - high.astype(jnp.float32)).astype(jnp.bfloat16)
    return high, low


def nt_dot(a, b):
    return lax.dot_general(a, b, (((1,), (1,)), ((), ())), preferred_element_type=jnp.float32)


def tn_dot(a, b):
    return lax.dot_general(a, b, (((0,), (0,)), ((), ())), preferred_element_type=jnp.float32)


def iota(shape, axis):
    return lax.broadcasted_iota(jnp.int32, shape, axis)


def kernel(
    n, nb, page_rows, w_chunks,
    own_hbm, tab_hbm, len_hbm, k_hbm, v_hbm, ck_hbm, cv_hbm, dq_hbm, dk_hbm, dv_hbm, q_hbm, w_hbm,
    out_ref, dec_ref,
    own_ref, tab_ref, len_ref, ck_ref, cv_ref, dq_ref, dk_ref, dv_ref, mix_ref, peak_ref, total_ref,
    kv, q_vm, w_vm, page_send, page_recv, count_send, count_recv, acc_all, stat_all,
    q8, dk8, dv8, y_send, y_recv,
    local_sem, ring_send, ring_recv, page_ss, page_rs, count_ss, count_rs,
    acc_ss, acc_rs, stat_ss, stat_rs, y_ss, y_rs,
):
    me = lax.axis_index("seq")
    mb = lax.axis_index("batch")
    mt = lax.axis_index("tp")
    tok = k_hbm.shape[1]
    kw = k_hbm.shape[2]
    k_heads = kw // HD
    q_heads = q_vm.shape[1] // HD
    group = q_heads // k_heads
    new, requests, _ = dq_ref.shape
    pages = tok // page_rows
    slots = tab_ref.shape[1]
    pool = ck_ref.shape[0]
    scaling = HD ** (-0.5)
    other = 1 - mt

    barrier = pltpu.get_barrier_semaphore()
    for k in range(1, n):
        pl.semaphore_signal(barrier, inc=1, device_id={"seq": lax.rem(me + k, n)}, device_id_type=pl.DeviceIdType.MESH)
    for k in range(1, nb):
        pl.semaphore_signal(barrier, inc=1, device_id={"batch": lax.rem(mb + k, nb)}, device_id_type=pl.DeviceIdType.MESH)
    pl.semaphore_signal(barrier, inc=1, device_id={"tp": other}, device_id_type=pl.DeviceIdType.MESH)

    mine = kv.at[me]
    sources = (
        (k_hbm.at[0], mine.at[:, pl.ds(0, kw)]), (v_hbm.at[0], mine.at[:, pl.ds(kw, kw)]), (own_hbm, own_ref),
        (dq_hbm, dq_ref), (dk_hbm, dk_ref), (dv_hbm, dv_ref), (tab_hbm, tab_ref), (len_hbm, len_ref),
        (ck_hbm, ck_ref), (cv_hbm, cv_ref), (q_hbm.at[0], q_vm), (w_hbm, w_vm))
    copies = [pltpu.make_async_copy(a, b, local_sem.at[i]) for i, (a, b) in enumerate(sources)]
    for copy in copies:
        copy.start()
    w_copy = copies.pop()
    q_copy = copies.pop()
    for copy in copies[:3]:
        copy.wait()

    owners = [own_ref[0, 0, j] for j in range(pages)]
    ranks = []
    for j in range(pages):
        rank = jnp.int32(0)
        for i in range(j):
            rank = rank + jnp.where(owners[i] == owners[j], 1, 0)
        ranks.append(rank)
    wide = MOST * page_rows
    source_page = iota((1, tok), 1) // page_rows
    place = jnp.zeros((1, tok), jnp.int32)
    for j in range(pages):
        place = jnp.where(source_page == j, owners[j] * MOST + ranks[j], place)
    row = iota((nb * wide, tok), 0)
    column = iota((nb * wide, tok), 1)
    chosen = (row // page_rows == place) & (row % page_rows == column % page_rows)
    chosen = jnp.where(chosen, 1.0, 0.0).astype(jnp.bfloat16)
    moved = jnp.dot(chosen, kv[me], preferred_element_type=jnp.float32)
    page_send[...] = moved.astype(jnp.bfloat16).reshape(nb, wide, 2 * kw)
    for o in range(nb):
        count = jnp.int32(0)
        for j in range(pages):
            count = count + jnp.where(owners[j] == o, 1, 0)
        count_send[o] = jnp.full((ROWS, LANES), count, jnp.int32)
    page_recv[mb] = page_send[mb]
    count_recv[mb] = count_send[mb]

    pl.semaphore_wait(barrier, (n - 1) + (nb - 1) + 1)

    def ring(i):
        block = me - i
        return pltpu.make_async_remote_copy(
            src_ref=kv.at[block], dst_ref=kv.at[block], send_sem=ring_send.at[i], recv_sem=ring_recv.at[i],
            device_id={"seq": me + 1}, device_id_type=pl.DeviceIdType.MESH)

    def arrival(i):
        block = me - 1 - i
        return pltpu.make_async_remote_copy(
            src_ref=kv.at[block], dst_ref=kv.at[block], send_sem=ring_send.at[i], recv_sem=ring_recv.at[i],
            device_id={"seq": me - 1}, device_id_type=pl.DeviceIdType.MESH)

    def page_pair(k):
        to = lax.rem(mb + k, nb)
        return (
            pltpu.make_async_remote_copy(
                src_ref=count_send.at[to], dst_ref=count_recv.at[mb], send_sem=count_ss.at[k - 1],
                recv_sem=count_rs.at[k - 1], device_id={"batch": to}, device_id_type=pl.DeviceIdType.MESH),
            pltpu.make_async_remote_copy(
                src_ref=page_send.at[to], dst_ref=page_recv.at[mb], send_sem=page_ss.at[k - 1],
                recv_sem=page_rs.at[k - 1], device_id={"batch": to}, device_id_type=pl.DeviceIdType.MESH),
        )

    def page_arrival(k):
        since = lax.rem(mb - k + nb, nb)
        return (
            pltpu.make_async_remote_copy(
                src_ref=count_send.at[since], dst_ref=count_recv.at[since], send_sem=count_ss.at[k - 1],
                recv_sem=count_rs.at[k - 1], device_id={"batch": since}, device_id_type=pl.DeviceIdType.MESH),
            pltpu.make_async_remote_copy(
                src_ref=page_send.at[since], dst_ref=page_recv.at[since], send_sem=page_ss.at[k - 1],
                recv_sem=page_rs.at[k - 1], device_id={"batch": since}, device_id_type=pl.DeviceIdType.MESH),
        )

    @pl.when(me < n - 1)
    def _():
        ring(0).start()

    for k in range(1, nb):
        for copy in page_pair(k):
            copy.start()

    def relay(i):
        @pl.when((me > i) & (me < n - 1))
        def _():
            arrival(i).wait_recv()
            ring(i + 1).start()

    def last_arrival(i):
        @pl.when(me == n - 1)
        def _():
            arrival(i).wait_recv()

    for copy in copies[3:]:
        copy.wait()

    for packed, ref in ((q8, dq_ref), (dk8, dk_ref), (dv8, dv_ref)):
        packed[...] = jnp.zeros_like(packed)
        for m in range(new):
            packed[m * requests:(m + 1) * requests, :] = ref[m]
    per_head = group * ROWS
    diagonal = []
    for a in range(k_heads):
        rows = jnp.concatenate(
            [q8[:, (a * group + g) * HD:(a * group + g + 1) * HD] for g in range(group)], axis=0)
        nothing = jnp.zeros((per_head, HD), jnp.float32)
        diagonal.append(jnp.concatenate([rows if b == a else nothing for b in range(k_heads)], axis=1))
    dec_q = jnp.concatenate(halves(jnp.concatenate(diagonal, axis=0)), axis=0)
    lanes = k_heads * per_head

    def dec_scores(keys):
        both = nt_dot(keys, dec_q)
        return (both[:, :lanes] + both[:, lanes:]) * scaling

    cache_rows = pool * page_rows
    token = iota((1, lanes), 1) % ROWS
    request = token % requests
    score_cache = dec_scores(ck_ref[...].reshape(cache_rows, kw))
    slot_of = iota((cache_rows, lanes), 0) // page_rows
    within = iota((cache_rows, lanes), 0) % page_rows
    live = jnp.zeros((cache_rows, lanes), jnp.int32)
    for r in range(requests):
        for j in range(slots):
            first = (j * n + me) * page_rows
            named = (slot_of == tab_ref[r, j]) & (request == r) & (first + within < len_ref[r])
            live = jnp.where(named, 1, live)
    score_cache = jnp.where(live > 0, score_cache, floor_score)
    new_k = jnp.concatenate([part.astype(jnp.float32) for part in halves(dk8[...])], axis=0).astype(jnp.bfloat16)
    new_v = jnp.concatenate([part.astype(jnp.float32) for part in halves(dv8[...])], axis=0).astype(jnp.bfloat16)
    score_new = dec_scores(new_k)
    score_new = score_new[:ROWS] + score_new[ROWS:]
    key_token = iota((ROWS, lanes), 0)
    causal = (key_token % requests == request) & (key_token <= token) & (me == 0)
    score_new = jnp.where(causal, score_new, floor_score)

    pair = 2
    pair_lanes = pair * tok
    sharpness = scaling * LOG2E
    visible = iota((tok, pair_lanes), 0) <= iota((tok, pair_lanes), 1) % tok

    def prefill_block(block, first):
        for a in range(k_heads):
            keys = kv[block, :, a * HD:(a + 1) * HD]
            values = kv[block, :, kw + a * HD:kw + (a + 1) * HD].T
            for p in range(group // pair):
                at = a * (group // pair) + p
                queries = jnp.concatenate(
                    [q_vm[:, (at * pair + i) * HD:(at * pair + i + 1) * HD] for i in range(pair)], axis=0)
                scores = nt_dot(keys, queries)
                if first:
                    scores = jnp.where(visible, scores, floor_score)
                high = jnp.max(scores, axis=0, keepdims=True)
                if not first:
                    before = peak_ref[at, 0:1, :]
                    high = jnp.maximum(high, before)
                weights = jnp.exp2((scores - high) * sharpness)
                sums = jnp.sum(weights, axis=0, keepdims=True)
                mixture = jnp.dot(values, weights.astype(jnp.bfloat16), preferred_element_type=jnp.float32)
                if not first:
                    shrink = jnp.exp2((before - high) * sharpness)
                    sums = sums + total_ref[at, 0:1, :] * shrink
                    mixture = mixture + mix_ref[at] * shrink
                peak_ref[at, 0:1, :] = high
                total_ref[at, 0:1, :] = sums
                mix_ref[at] = mixture

    q_copy.wait()
    prefill_block(me, True)
    relay(0)

    for k in range(1, nb):
        for copy in page_arrival(k):
            copy.wait_recv()
    received = page_recv[...].reshape(nb * wide, 2 * kw)
    score_recv = dec_scores(received[:, :kw])
    place_of = iota((wide, lanes), 0) // page_rows
    kept = jnp.concatenate([jnp.where(place_of < count_recv[b][0:1, :], 1, 0) for b in range(nb)], axis=0)
    score_recv = jnp.where(kept > 0, score_recv, floor_score)
    peak = jnp.maximum(
        jnp.maximum(jnp.max(score_cache, axis=0, keepdims=True), jnp.max(score_recv, axis=0, keepdims=True)),
        jnp.max(score_new, axis=0, keepdims=True))
    weight_cache = jnp.where(live > 0, jnp.exp(score_cache - peak), 0.0)
    weight_recv = jnp.where(kept > 0, jnp.exp(score_recv - peak), 0.0)
    weight_new = jnp.where(causal, jnp.exp(score_new - peak), 0.0)
    total = (jnp.sum(weight_cache, axis=0, keepdims=True) + jnp.sum(weight_recv, axis=0, keepdims=True)
             + jnp.sum(weight_new, axis=0, keepdims=True))

    def dec_values(values, weights):
        both = tn_dot(values, jnp.concatenate(halves(weights), axis=1))
        return both[:, :lanes] + both[:, lanes:]

    mixed = dec_values(cv_ref[...].reshape(cache_rows, kw), weight_cache)
    mixed = mixed + dec_values(received[:, kw:], weight_recv)
    mixed = mixed + dec_values(new_v, jnp.concatenate([weight_new, weight_new], axis=0))
    lane_head = iota((HD, lanes), 1) // per_head
    acc = mixed[0:HD]
    for a in range(1, k_heads):
        acc = jnp.where(lane_head == a, mixed[a * HD:(a + 1) * HD], acc)
    acc_all[me] = acc.astype(jnp.bfloat16)
    stat_row = iota((ROWS, lanes), 0)
    stat_all[me] = jnp.where(stat_row == 0, peak, total)

    def partial_pair(k, slot, to):
        return (
            pltpu.make_async_remote_copy(
                src_ref=acc_all.at[slot], dst_ref=acc_all.at[slot], send_sem=acc_ss.at[k - 1],
                recv_sem=acc_rs.at[k - 1], device_id={"seq": to}, device_id_type=pl.DeviceIdType.MESH),
            pltpu.make_async_remote_copy(
                src_ref=stat_all.at[slot], dst_ref=stat_all.at[slot], send_sem=stat_ss.at[k - 1],
                recv_sem=stat_rs.at[k - 1], device_id={"seq": to}, device_id_type=pl.DeviceIdType.MESH),
        )

    for k in range(1, n):
        for copy in partial_pair(k, me, lax.rem(me + k, n)):
            copy.start()

    last_arrival(0)

    @pl.when(me >= 1)
    def _():
        prefill_block(me - 1, False)

    if n > 2:
        relay(1)
        last_arrival(1)

        @pl.when(me >= 2)
        def _():
            prefill_block(me - 2, False)

    for k in range(1, n):
        since = lax.rem(me - k + n, n)
        for copy in partial_pair(k, since, since):
            copy.wait_recv()
    peaks = [stat_all[s][0:1, :] for s in range(n)]
    top = functools.reduce(jnp.maximum, peaks)
    scales = [jnp.exp(p - top) for p in peaks]
    whole = sum(stat_all[s][1:2, :] * scales[s] for s in range(n))
    merged = sum(acc_all[s].astype(jnp.float32) * scales[s] for s in range(n)) / whole
    merged = merged.T
    attention = jnp.concatenate([merged[h * ROWS:(h + 1) * ROWS] for h in range(q_heads)], axis=1)
    parts = jnp.concatenate([p.astype(jnp.float32) for p in halves(attention)], axis=0).astype(jnp.bfloat16)
    w_copy.wait()
    step = w_vm.shape[1] // w_chunks

    def y_copy(c):
        return pltpu.make_async_remote_copy(
            src_ref=y_send.at[c], dst_ref=y_recv.at[c], send_sem=y_ss.at[c], recv_sem=y_rs.at[c],
            device_id={"tp": other}, device_id_type=pl.DeviceIdType.MESH)

    for c in range(w_chunks):
        both = jnp.dot(parts, w_vm[:, c * step:(c + 1) * step], preferred_element_type=jnp.float32)
        y_send[c] = both[:ROWS] + both[ROWS:]
        y_copy(c).start()

    def later(i, carry):
        @pl.when(me >= i)
        def _():
            arrival(i - 1).wait_recv()

            @pl.when(me < n - 1)
            def _():
                ring(i).start()

            prefill_block(me - i, False)
        return carry

    lax.fori_loop(3, n, later, 0)

    unit = jnp.where(iota((tok, tok), 0) == iota((tok, tok), 1), 1.0, 0.0).astype(jnp.bfloat16)
    for at in range(q_heads // pair):
        done = (mix_ref[at] * (1.0 / total_ref[at, 0:1, :])).astype(jnp.bfloat16)
        for i in range(pair):
            turned = nt_dot(unit, done[:, i * tok:(i + 1) * tok])
            head = at * pair + i
            out_ref[0, :, head * HD:(head + 1) * HD] = turned.astype(jnp.bfloat16)

    for c in range(w_chunks):
        y_copy(c).wait()
        y = y_send[c] + y_recv[c]
        for m in range(new):
            dec_ref[m, :, c * step:(c + 1) * step] = y[m * requests:(m + 1) * requests]

    for i in range(n - 1):
        @pl.when((me < n - 1) & (me >= i))
        def _():
            ring(i).wait_send()
    for k in range(1, nb):
        for copy in page_pair(k):
            copy.wait_send()
    for k in range(1, n):
        for copy in partial_pair(k, me, lax.rem(me + k, n)):
            copy.wait_send()


def hand_over(pre_ref, dec_ref, pre_hbm, dec_hbm, sems):
    copies = [
        pltpu.make_async_copy(a, b, sems.at[i]) for i, (a, b) in enumerate(((pre_ref, pre_hbm), (dec_ref, dec_hbm)))]
    for copy in copies:
        copy.start()
    for copy in copies:
        copy.wait()


def local(
    pre_q, pre_k, pre_v, owner_map, cache_k, cache_v, tables, lengths, dec_q, dec_k, dec_v, w_out
):
    n = lax.axis_size("seq")
    nb = lax.axis_size("batch")
    tok = pre_q.shape[1]
    kw = pre_k.shape[2]
    page_rows = cache_k.shape[1]
    lanes = pre_q.shape[2] // HD * ROWS
    out_columns = w_out.shape[1]
    w_chunks = max(1, out_columns // 512)
    vmem = pl.BlockSpec(memory_space=pltpu.VMEM)
    hbm = pl.BlockSpec(memory_space=pltpu.HBM)
    dma = pltpu.SemaphoreType.DMA
    pre_out, dec_out = pl.pallas_call(
        functools.partial(kernel, n, nb, page_rows, w_chunks),
        out_shape=(
            pltpu.VMEM(pre_q.shape, jnp.bfloat16),
            pltpu.VMEM((dec_q.shape[1], dec_q.shape[0], out_columns), jnp.float32),
        ),
        in_specs=[hbm] * 12,
        out_specs=(vmem, vmem),
        scratch_shapes=[
            pltpu.SMEM((1, 1, owner_map.shape[1]), jnp.int32),
            pltpu.SMEM(tables.shape, jnp.int32),
            pltpu.SMEM(lengths.shape, jnp.int32),
            pltpu.VMEM(cache_k.shape, jnp.bfloat16),
            pltpu.VMEM(cache_v.shape, jnp.bfloat16),
            pltpu.VMEM((dec_q.shape[1], dec_q.shape[0], dec_q.shape[2]), jnp.float32),
            pltpu.VMEM((dec_q.shape[1], dec_q.shape[0], kw), jnp.float32),
            pltpu.VMEM((dec_q.shape[1], dec_q.shape[0], kw), jnp.float32),
            pltpu.VMEM((lanes // (2 * ROWS), HD, 2 * tok), jnp.float32),
            pltpu.VMEM((lanes // (2 * ROWS), ROWS, 2 * tok), jnp.float32),
            pltpu.VMEM((lanes // (2 * ROWS), ROWS, 2 * tok), jnp.float32),
            pltpu.VMEM((n, tok, 2 * kw), jnp.bfloat16),
            pltpu.VMEM((tok, pre_q.shape[2]), jnp.bfloat16),
            pltpu.VMEM(w_out.shape, jnp.bfloat16),
            pltpu.VMEM((nb, MOST * page_rows, 2 * kw), jnp.bfloat16),
            pltpu.VMEM((nb, MOST * page_rows, 2 * kw), jnp.bfloat16),
            pltpu.VMEM((nb, ROWS, LANES), jnp.int32),
            pltpu.VMEM((nb, ROWS, LANES), jnp.int32),
            pltpu.VMEM((n, HD, lanes), jnp.bfloat16),
            pltpu.VMEM((n, ROWS, lanes), jnp.float32),
            pltpu.VMEM((ROWS, dec_q.shape[2]), jnp.float32),
            pltpu.VMEM((ROWS, kw), jnp.float32),
            pltpu.VMEM((ROWS, kw), jnp.float32),
            pltpu.VMEM((w_chunks, ROWS, out_columns // w_chunks), jnp.float32),
            pltpu.VMEM((w_chunks, ROWS, out_columns // w_chunks), jnp.float32),
            dma((12,)),
            dma((n - 1,)), dma((n - 1,)),
            dma((nb - 1,)), dma((nb - 1,)), dma((nb - 1,)), dma((nb - 1,)),
            dma((n - 1,)), dma((n - 1,)), dma((n - 1,)), dma((n - 1,)),
            dma((w_chunks,)), dma((w_chunks,)),
        ],
        compiler_params=pltpu.CompilerParams(
            collective_id=0, has_side_effects=True, vmem_limit_bytes=48 * 1024 * 1024
        ),
        name="prefill_and_decode",
    )(*(pltpu.with_memory_space_constraint(x, pltpu.HBM) for x in (
        jnp.swapaxes(owner_map, 1, 2), tables, lengths, pre_k, pre_v, cache_k, cache_v,
        *(jnp.swapaxes(x, 0, 1) for x in (dec_q, dec_k, dec_v)), pre_q, w_out,
    )))
    pre_out, dec_out = pl.pallas_call(
        hand_over,
        out_shape=(pltpu.HBM(pre_out.shape, pre_out.dtype), pltpu.HBM(dec_out.shape, dec_out.dtype)),
        in_specs=[vmem] * 2,
        out_specs=(hbm, hbm),
        scratch_shapes=[dma((2,))],
        name="hand_over",
    )(*(pltpu.with_memory_space_constraint(x, pltpu.VMEM) for x in (pre_out, dec_out)))
    return pre_out, jnp.swapaxes(dec_out, 0, 1)


def solution(mesh):
    placed = (
        P("batch", "seq", "tp"),
        P("batch", "seq", "tp"),
        P("batch", "seq", "tp"),
        P("batch", "seq", None),
        P("batch", "seq", "tp"),
        P("batch", "seq", "tp"),
        P("batch", "seq"),
        P("batch"),
        P("batch", None, "tp"),
        P("batch", None, "tp"),
        P("batch", None, "tp"),
        P("tp", "seq"),
    )
    return jax.shard_map(
        local,
        mesh=mesh,
        in_specs=placed,
        out_specs=(P("batch", "seq", "tp"), P("batch", None, "seq")),
        check_vma=False,
    )
```

```python
import functools

import jax
import jax.numpy as jnp
from jax import lax
from jax.experimental import pallas as pl
from jax.experimental.pallas import tpu as pltpu
from jax.sharding import PartitionSpec as P

HD = 128
MOST = 4
ROWS = 8
LANES = 128
floor_score = -1e30
LOG2E = 1.4426950408889634


def halves(x):
    high = x.astype(jnp.bfloat16)
    low = (x - high.astype(jnp.float32)).astype(jnp.bfloat16)
    return high, low


def nt_dot(a, b):
    return lax.dot_general(a, b, (((1,), (1,)), ((), ())), preferred_element_type=jnp.float32)


def tn_dot(a, b):
    return lax.dot_general(a, b, (((0,), (0,)), ((), ())), preferred_element_type=jnp.float32)


def iota(shape, axis):
    return lax.broadcasted_iota(jnp.int32, shape, axis)


def kernel(
    n, nb, page_rows, w_chunks,
    own_hbm, tab_hbm, len_hbm, k_hbm, v_hbm, ck_hbm, cv_hbm, dq_hbm, dk_hbm, dv_hbm, q_hbm, w_hbm,
    out_ref, dec_ref,
    own_ref, tab_ref, len_ref, ck_ref, cv_ref, dq_ref, dk_ref, dv_ref, mix_ref, peak_ref, total_ref,
    kv, q_vm, w_vm, page_send, page_recv, count_send, count_recv, acc_all, stat_all,
    q8, dk8, dv8, y_send, y_recv,
    local_sem, ring_send, ring_recv, page_ss, page_rs, count_ss, count_rs,
    acc_ss, acc_rs, stat_ss, stat_rs, y_ss, y_rs,
):
    me = lax.axis_index("seq")
    mb = lax.axis_index("batch")
    mt = lax.axis_index("tp")
    tok = k_hbm.shape[1]
    kw = k_hbm.shape[2]
    k_heads = kw // HD
    q_heads = q_vm.shape[1] // HD
    group = q_heads // k_heads
    new, requests, _ = dq_ref.shape
    pages = tok // page_rows
    slots = tab_ref.shape[1]
    pool = ck_ref.shape[0]
    scaling = HD ** (-0.5)
    other = 1 - mt

    barrier = pltpu.get_barrier_semaphore()
    for k in range(1, n):
        pl.semaphore_signal(barrier, inc=1, device_id={"seq": lax.rem(me + k, n)}, device_id_type=pl.DeviceIdType.MESH)
    for k in range(1, nb):
        pl.semaphore_signal(barrier, inc=1, device_id={"batch": lax.rem(mb + k, nb)}, device_id_type=pl.DeviceIdType.MESH)
    pl.semaphore_signal(barrier, inc=1, device_id={"tp": other}, device_id_type=pl.DeviceIdType.MESH)

    mine = kv.at[me]
    sources = (
        (k_hbm.at[0], mine.at[:, pl.ds(0, kw)]), (v_hbm.at[0], mine.at[:, pl.ds(kw, kw)]), (own_hbm, own_ref),
        (dq_hbm, dq_ref), (dk_hbm, dk_ref), (dv_hbm, dv_ref), (tab_hbm, tab_ref), (len_hbm, len_ref),
        (ck_hbm, ck_ref), (cv_hbm, cv_ref), (q_hbm.at[0], q_vm), (w_hbm, w_vm))
    copies = [pltpu.make_async_copy(a, b, local_sem.at[i]) for i, (a, b) in enumerate(sources)]
    for copy in copies:
        copy.start()
    w_copy = copies.pop()
    q_copy = copies.pop()
    for copy in copies[:3]:
        copy.wait()

    owners = [own_ref[0, 0, j] for j in range(pages)]
    ranks = []
    for j in range(pages):
        rank = jnp.int32(0)
        for i in range(j):
            rank = rank + jnp.where(owners[i] == owners[j], 1, 0)
        ranks.append(rank)
    wide = MOST * page_rows
    source_page = iota((1, tok), 1) // page_rows
    place = jnp.zeros((1, tok), jnp.int32)
    for j in range(pages):
        place = jnp.where(source_page == j, owners[j] * MOST + ranks[j], place)
    row = iota((nb * wide, tok), 0)
    column = iota((nb * wide, tok), 1)
    chosen = (row // page_rows == place) & (row % page_rows == column % page_rows)
    chosen = jnp.where(chosen, 1.0, 0.0).astype(jnp.bfloat16)
    moved = jnp.dot(chosen, kv[me], preferred_element_type=jnp.float32)
    page_send[...] = moved.astype(jnp.bfloat16).reshape(nb, wide, 2 * kw)
    for o in range(nb):
        count = jnp.int32(0)
        for j in range(pages):
            count = count + jnp.where(owners[j] == o, 1, 0)
        count_send[o] = jnp.full((ROWS, LANES), count, jnp.int32)
    page_recv[mb] = page_send[mb]
    count_recv[mb] = count_send[mb]

    pl.semaphore_wait(barrier, (n - 1) + (nb - 1) + 1)

    def ring(i):
        block = me - i
        return pltpu.make_async_remote_copy(
            src_ref=kv.at[block], dst_ref=kv.at[block], send_sem=ring_send.at[i], recv_sem=ring_recv.at[i],
            device_id={"seq": me + 1}, device_id_type=pl.DeviceIdType.MESH)

    def arrival(i):
        block = me - 1 - i
        return pltpu.make_async_remote_copy(
            src_ref=kv.at[block], dst_ref=kv.at[block], send_sem=ring_send.at[i], recv_sem=ring_recv.at[i],
            device_id={"seq": me - 1}, device_id_type=pl.DeviceIdType.MESH)

    def page_pair(k):
        to = lax.rem(mb + k, nb)
        return (
            pltpu.make_async_remote_copy(
                src_ref=count_send.at[to], dst_ref=count_recv.at[mb], send_sem=count_ss.at[k - 1],
                recv_sem=count_rs.at[k - 1], device_id={"batch": to}, device_id_type=pl.DeviceIdType.MESH),
            pltpu.make_async_remote_copy(
                src_ref=page_send.at[to], dst_ref=page_recv.at[mb], send_sem=page_ss.at[k - 1],
                recv_sem=page_rs.at[k - 1], device_id={"batch": to}, device_id_type=pl.DeviceIdType.MESH),
        )

    def page_arrival(k):
        since = lax.rem(mb - k + nb, nb)
        return (
            pltpu.make_async_remote_copy(
                src_ref=count_send.at[since], dst_ref=count_recv.at[since], send_sem=count_ss.at[k - 1],
                recv_sem=count_rs.at[k - 1], device_id={"batch": since}, device_id_type=pl.DeviceIdType.MESH),
            pltpu.make_async_remote_copy(
                src_ref=page_send.at[since], dst_ref=page_recv.at[since], send_sem=page_ss.at[k - 1],
                recv_sem=page_rs.at[k - 1], device_id={"batch": since}, device_id_type=pl.DeviceIdType.MESH),
        )

    even = lax.rem(me, 2) == 0

    def two_up():
        return pltpu.make_async_remote_copy(
            src_ref=kv.at[me], dst_ref=kv.at[me], send_sem=ring_send.at[n - 1], recv_sem=ring_recv.at[1],
            device_id={"seq": me + 2}, device_id_type=pl.DeviceIdType.MESH)

    @pl.when(me < n - 1)
    def _():
        ring(0).start()

    @pl.when(even & (me < n - 2))
    def _():
        two_up().start()

    for k in range(1, nb):
        for copy in page_pair(k):
            copy.start()

    def relay(i):
        @pl.when((me > i) & (me < n - 1) & (even | (i > 0)))
        def _():
            arrival(i).wait_recv()
            ring(i + 1).start()

    def final_arrival(i):
        @pl.when((me > i) & ((me == n - 1) | (~even & (i == 0))))
        def _():
            arrival(i).wait_recv()

    for copy in copies[3:]:
        copy.wait()

    for packed, ref in ((q8, dq_ref), (dk8, dk_ref), (dv8, dv_ref)):
        packed[...] = jnp.zeros_like(packed)
        for m in range(new):
            packed[m * requests:(m + 1) * requests, :] = ref[m]
    per_head = group * ROWS
    diagonal = []
    for a in range(k_heads):
        rows = jnp.concatenate(
            [q8[:, (a * group + g) * HD:(a * group + g + 1) * HD] for g in range(group)], axis=0)
        nothing = jnp.zeros((per_head, HD), jnp.float32)
        diagonal.append(jnp.concatenate([rows if b == a else nothing for b in range(k_heads)], axis=1))
    dec_q = jnp.concatenate(halves(jnp.concatenate(diagonal, axis=0)), axis=0)
    lanes = k_heads * per_head

    def dec_scores(keys):
        both = nt_dot(keys, dec_q)
        return (both[:, :lanes] + both[:, lanes:]) * scaling

    cache_rows = pool * page_rows
    token = iota((1, lanes), 1) % ROWS
    request = token % requests
    score_cache = dec_scores(ck_ref[...].reshape(cache_rows, kw))
    slot_of = iota((cache_rows, lanes), 0) // page_rows
    within = iota((cache_rows, lanes), 0) % page_rows
    live = jnp.zeros((cache_rows, lanes), jnp.int32)
    for r in range(requests):
        for j in range(slots):
            first = (j * n + me) * page_rows
            named = (slot_of == tab_ref[r, j]) & (request == r) & (first + within < len_ref[r])
            live = jnp.where(named, 1, live)
    score_cache = jnp.where(live > 0, score_cache, floor_score)
    new_k = jnp.concatenate([part.astype(jnp.float32) for part in halves(dk8[...])], axis=0).astype(jnp.bfloat16)
    new_v = jnp.concatenate([part.astype(jnp.float32) for part in halves(dv8[...])], axis=0).astype(jnp.bfloat16)
    score_new = dec_scores(new_k)
    score_new = score_new[:ROWS] + score_new[ROWS:]
    key_token = iota((ROWS, lanes), 0)
    causal = (key_token % requests == request) & (key_token <= token) & (me == 0)
    score_new = jnp.where(causal, score_new, floor_score)

    pair = 2
    pair_lanes = pair * tok
    sharpness = scaling * LOG2E
    visible = iota((tok, pair_lanes), 0) <= iota((tok, pair_lanes), 1) % tok

    def prefill_block(block, first):
        for a in range(k_heads):
            keys = kv[block, :, a * HD:(a + 1) * HD]
            values = kv[block, :, kw + a * HD:kw + (a + 1) * HD].T
            for p in range(group // pair):
                at = a * (group // pair) + p
                queries = jnp.concatenate(
                    [q_vm[:, (at * pair + i) * HD:(at * pair + i + 1) * HD] for i in range(pair)], axis=0)
                scores = nt_dot(keys, queries)
                if first:
                    scores = jnp.where(visible, scores, floor_score)
                high = jnp.max(scores, axis=0, keepdims=True)
                if not first:
                    before = peak_ref[at, 0:1, :]
                    high = jnp.maximum(high, before)
                weights = jnp.exp2((scores - high) * sharpness)
                sums = jnp.sum(weights, axis=0, keepdims=True)
                mixture = jnp.dot(values, weights.astype(jnp.bfloat16), preferred_element_type=jnp.float32)
                if not first:
                    shrink = jnp.exp2((before - high) * sharpness)
                    sums = sums + total_ref[at, 0:1, :] * shrink
                    mixture = mixture + mix_ref[at] * shrink
                peak_ref[at, 0:1, :] = high
                total_ref[at, 0:1, :] = sums
                mix_ref[at] = mixture

    q_copy.wait()
    prefill_block(me, True)
    relay(0)

    for k in range(1, nb):
        for copy in page_arrival(k):
            copy.wait_recv()
    received = page_recv[...].reshape(nb * wide, 2 * kw)
    score_recv = dec_scores(received[:, :kw])
    place_of = iota((wide, lanes), 0) // page_rows
    kept = jnp.concatenate([jnp.where(place_of < count_recv[b][0:1, :], 1, 0) for b in range(nb)], axis=0)
    score_recv = jnp.where(kept > 0, score_recv, floor_score)
    peak = jnp.maximum(
        jnp.maximum(jnp.max(score_cache, axis=0, keepdims=True), jnp.max(score_recv, axis=0, keepdims=True)),
        jnp.max(score_new, axis=0, keepdims=True))
    weight_cache = jnp.where(live > 0, jnp.exp(score_cache - peak), 0.0)
    weight_recv = jnp.where(kept > 0, jnp.exp(score_recv - peak), 0.0)
    weight_new = jnp.where(causal, jnp.exp(score_new - peak), 0.0)
    total = (jnp.sum(weight_cache, axis=0, keepdims=True) + jnp.sum(weight_recv, axis=0, keepdims=True)
             + jnp.sum(weight_new, axis=0, keepdims=True))

    def dec_values(values, weights):
        both = tn_dot(values, jnp.concatenate(halves(weights), axis=1))
        return both[:, :lanes] + both[:, lanes:]

    mixed = dec_values(cv_ref[...].reshape(cache_rows, kw), weight_cache)
    mixed = mixed + dec_values(received[:, kw:], weight_recv)
    mixed = mixed + dec_values(new_v, jnp.concatenate([weight_new, weight_new], axis=0))
    lane_head = iota((HD, lanes), 1) // per_head
    acc = mixed[0:HD]
    for a in range(1, k_heads):
        acc = jnp.where(lane_head == a, mixed[a * HD:(a + 1) * HD], acc)
    acc_all[me] = acc.astype(jnp.bfloat16)
    stat_row = iota((ROWS, lanes), 0)
    stat_all[me] = jnp.where(stat_row == 0, peak, total)

    def partial_pair(k, slot, to):
        return (
            pltpu.make_async_remote_copy(
                src_ref=acc_all.at[slot], dst_ref=acc_all.at[slot], send_sem=acc_ss.at[k - 1],
                recv_sem=acc_rs.at[k - 1], device_id={"seq": to}, device_id_type=pl.DeviceIdType.MESH),
            pltpu.make_async_remote_copy(
                src_ref=stat_all.at[slot], dst_ref=stat_all.at[slot], send_sem=stat_ss.at[k - 1],
                recv_sem=stat_rs.at[k - 1], device_id={"seq": to}, device_id_type=pl.DeviceIdType.MESH),
        )

    for k in range(1, n):
        for copy in partial_pair(k, me, lax.rem(me + k, n)):
            copy.start()

    if n > 2:
        relay(1)
    final_arrival(0)

    @pl.when(me >= 1)
    def _():
        prefill_block(me - 1, False)

    if n > 2:
        final_arrival(1)

        @pl.when(me >= 2)
        def _():
            prefill_block(me - 2, False)

    for k in range(1, n):
        since = lax.rem(me - k + n, n)
        for copy in partial_pair(k, since, since):
            copy.wait_recv()
    peaks = [stat_all[s][0:1, :] for s in range(n)]
    top = functools.reduce(jnp.maximum, peaks)
    scales = [jnp.exp(p - top) for p in peaks]
    whole = sum(stat_all[s][1:2, :] * scales[s] for s in range(n))
    merged = sum(acc_all[s].astype(jnp.float32) * scales[s] for s in range(n)) / whole
    merged = merged.T
    attention = jnp.concatenate([merged[h * ROWS:(h + 1) * ROWS] for h in range(q_heads)], axis=1)
    parts = jnp.concatenate([p.astype(jnp.float32) for p in halves(attention)], axis=0).astype(jnp.bfloat16)
    w_copy.wait()
    step = w_vm.shape[1] // w_chunks

    def y_copy(c):
        return pltpu.make_async_remote_copy(
            src_ref=y_send.at[c], dst_ref=y_recv.at[c], send_sem=y_ss.at[c], recv_sem=y_rs.at[c],
            device_id={"tp": other}, device_id_type=pl.DeviceIdType.MESH)

    for c in range(w_chunks):
        both = jnp.dot(parts, w_vm[:, c * step:(c + 1) * step], preferred_element_type=jnp.float32)
        y_send[c] = both[:ROWS] + both[ROWS:]
        y_copy(c).start()

    def later(i, carry):
        @pl.when(me >= i)
        def _():
            arrival(i - 1).wait_recv()

            @pl.when(me < n - 1)
            def _():
                ring(i).start()

            prefill_block(me - i, False)
        return carry

    lax.fori_loop(3, n, later, 0)

    unit = jnp.where(iota((tok, tok), 0) == iota((tok, tok), 1), 1.0, 0.0).astype(jnp.bfloat16)
    for at in range(q_heads // pair):
        done = (mix_ref[at] * (1.0 / total_ref[at, 0:1, :])).astype(jnp.bfloat16)
        for i in range(pair):
            turned = nt_dot(unit, done[:, i * tok:(i + 1) * tok])
            head = at * pair + i
            out_ref[0, :, head * HD:(head + 1) * HD] = turned.astype(jnp.bfloat16)

    for c in range(w_chunks):
        y_copy(c).wait()
        y = y_send[c] + y_recv[c]
        for m in range(new):
            dec_ref[m, :, c * step:(c + 1) * step] = y[m * requests:(m + 1) * requests]

    for i in range(n - 1):
        @pl.when((me < n - 1) & (me >= i) & (even | (i != 1)))
        def _():
            ring(i).wait_send()

    @pl.when(even & (me < n - 2))
    def _():
        two_up().wait_send()
    for k in range(1, nb):
        for copy in page_pair(k):
            copy.wait_send()
    for k in range(1, n):
        for copy in partial_pair(k, me, lax.rem(me + k, n)):
            copy.wait_send()


def hand_over(pre_ref, dec_ref, pre_hbm, dec_hbm, sems):
    copies = [
        pltpu.make_async_copy(a, b, sems.at[i]) for i, (a, b) in enumerate(((pre_ref, pre_hbm), (dec_ref, dec_hbm)))]
    for copy in copies:
        copy.start()
    for copy in copies:
        copy.wait()


def local(
    pre_q, pre_k, pre_v, owner_map, cache_k, cache_v, tables, lengths, dec_q, dec_k, dec_v, w_out
):
    n = lax.axis_size("seq")
    nb = lax.axis_size("batch")
    tok = pre_q.shape[1]
    kw = pre_k.shape[2]
    page_rows = cache_k.shape[1]
    lanes = pre_q.shape[2] // HD * ROWS
    out_columns = w_out.shape[1]
    w_chunks = max(1, out_columns // 512)
    vmem = pl.BlockSpec(memory_space=pltpu.VMEM)
    hbm = pl.BlockSpec(memory_space=pltpu.HBM)
    dma = pltpu.SemaphoreType.DMA
    pre_out, dec_out = pl.pallas_call(
        functools.partial(kernel, n, nb, page_rows, w_chunks),
        out_shape=(
            pltpu.VMEM(pre_q.shape, jnp.bfloat16),
            pltpu.VMEM((dec_q.shape[1], dec_q.shape[0], out_columns), jnp.float32),
        ),
        in_specs=[hbm] * 12,
        out_specs=(vmem, vmem),
        scratch_shapes=[
            pltpu.SMEM((1, 1, owner_map.shape[1]), jnp.int32),
            pltpu.SMEM(tables.shape, jnp.int32),
            pltpu.SMEM(lengths.shape, jnp.int32),
            pltpu.VMEM(cache_k.shape, jnp.bfloat16),
            pltpu.VMEM(cache_v.shape, jnp.bfloat16),
            pltpu.VMEM((dec_q.shape[1], dec_q.shape[0], dec_q.shape[2]), jnp.float32),
            pltpu.VMEM((dec_q.shape[1], dec_q.shape[0], kw), jnp.float32),
            pltpu.VMEM((dec_q.shape[1], dec_q.shape[0], kw), jnp.float32),
            pltpu.VMEM((lanes // (2 * ROWS), HD, 2 * tok), jnp.float32),
            pltpu.VMEM((lanes // (2 * ROWS), ROWS, 2 * tok), jnp.float32),
            pltpu.VMEM((lanes // (2 * ROWS), ROWS, 2 * tok), jnp.float32),
            pltpu.VMEM((n, tok, 2 * kw), jnp.bfloat16),
            pltpu.VMEM((tok, pre_q.shape[2]), jnp.bfloat16),
            pltpu.VMEM(w_out.shape, jnp.bfloat16),
            pltpu.VMEM((nb, MOST * page_rows, 2 * kw), jnp.bfloat16),
            pltpu.VMEM((nb, MOST * page_rows, 2 * kw), jnp.bfloat16),
            pltpu.VMEM((nb, ROWS, LANES), jnp.int32),
            pltpu.VMEM((nb, ROWS, LANES), jnp.int32),
            pltpu.VMEM((n, HD, lanes), jnp.bfloat16),
            pltpu.VMEM((n, ROWS, lanes), jnp.float32),
            pltpu.VMEM((ROWS, dec_q.shape[2]), jnp.float32),
            pltpu.VMEM((ROWS, kw), jnp.float32),
            pltpu.VMEM((ROWS, kw), jnp.float32),
            pltpu.VMEM((w_chunks, ROWS, out_columns // w_chunks), jnp.float32),
            pltpu.VMEM((w_chunks, ROWS, out_columns // w_chunks), jnp.float32),
            dma((12,)),
            dma((n,)), dma((n - 1,)),
            dma((nb - 1,)), dma((nb - 1,)), dma((nb - 1,)), dma((nb - 1,)),
            dma((n - 1,)), dma((n - 1,)), dma((n - 1,)), dma((n - 1,)),
            dma((w_chunks,)), dma((w_chunks,)),
        ],
        compiler_params=pltpu.CompilerParams(
            collective_id=0, has_side_effects=True, vmem_limit_bytes=48 * 1024 * 1024
        ),
        name="prefill_and_decode",
    )(*(pltpu.with_memory_space_constraint(x, pltpu.HBM) for x in (
        jnp.swapaxes(owner_map, 1, 2), tables, lengths, pre_k, pre_v, cache_k, cache_v,
        *(jnp.swapaxes(x, 0, 1) for x in (dec_q, dec_k, dec_v)), pre_q, w_out,
    )))
    pre_out, dec_out = pl.pallas_call(
        hand_over,
        out_shape=(pltpu.HBM(pre_out.shape, pre_out.dtype), pltpu.HBM(dec_out.shape, dec_out.dtype)),
        in_specs=[vmem] * 2,
        out_specs=(hbm, hbm),
        scratch_shapes=[dma((2,))],
        name="hand_over",
    )(*(pltpu.with_memory_space_constraint(x, pltpu.VMEM) for x in (pre_out, dec_out)))
    return pre_out, jnp.swapaxes(dec_out, 0, 1)


def solution(mesh):
    placed = (
        P("batch", "seq", "tp"),
        P("batch", "seq", "tp"),
        P("batch", "seq", "tp"),
        P("batch", "seq", None),
        P("batch", "seq", "tp"),
        P("batch", "seq", "tp"),
        P("batch", "seq"),
        P("batch"),
        P("batch", None, "tp"),
        P("batch", None, "tp"),
        P("batch", None, "tp"),
        P("tp", "seq"),
    )
    return jax.shard_map(
        local,
        mesh=mesh,
        in_specs=placed,
        out_specs=(P("batch", "seq", "tp"), P("batch", None, "seq")),
        check_vma=False,
    )
```

```python
import functools

import jax
import jax.numpy as jnp
from jax import lax
from jax.experimental import pallas as pl
from jax.experimental.pallas import tpu as pltpu
from jax.sharding import PartitionSpec as P

HD = 128
MOST = 4
ROWS = 8
LANES = 128
floor_score = -1e30
LOG2E = 1.4426950408889634


def halves(x):
    high = x.astype(jnp.bfloat16)
    low = (x - high.astype(jnp.float32)).astype(jnp.bfloat16)
    return high, low


def nt_dot(a, b):
    return lax.dot_general(a, b, (((1,), (1,)), ((), ())), preferred_element_type=jnp.float32)


def tn_dot(a, b):
    return lax.dot_general(a, b, (((0,), (0,)), ((), ())), preferred_element_type=jnp.float32)


def iota(shape, axis):
    return lax.broadcasted_iota(jnp.int32, shape, axis)


def kernel(
    n, nb, page_rows, w_chunks,
    own_hbm, tab_hbm, len_hbm, k_hbm, v_hbm, ck_hbm, cv_hbm, dq_hbm, dk_hbm, dv_hbm, q_hbm, w_hbm,
    out_ref, dec_ref,
    own_ref, tab_ref, len_ref, ck_ref, cv_ref, dq_ref, dk_ref, dv_ref, mix_ref, peak_ref, total_ref,
    kv, q_vm, w_vm, page_send, page_recv, count_send, count_recv, acc_all, stat_all,
    q8, dk8, dv8, y_send, y_recv,
    local_sem, ring_send, ring_recv, page_ss, page_rs, count_ss, count_rs,
    acc_ss, acc_rs, stat_ss, stat_rs, y_ss, y_rs,
):
    me = lax.axis_index("seq")
    mb = lax.axis_index("batch")
    mt = lax.axis_index("tp")
    tok = k_hbm.shape[1]
    kw = k_hbm.shape[2]
    k_heads = kw // HD
    q_heads = q_vm.shape[1] // HD
    group = q_heads // k_heads
    new, requests, _ = dq_ref.shape
    pages = tok // page_rows
    slots = tab_ref.shape[1]
    pool = ck_ref.shape[0]
    scaling = HD ** (-0.5)
    other = 1 - mt

    barrier = pltpu.get_barrier_semaphore()
    for k in range(1, n):
        pl.semaphore_signal(barrier, inc=1, device_id={"seq": lax.rem(me + k, n)}, device_id_type=pl.DeviceIdType.MESH)
    for k in range(1, nb):
        pl.semaphore_signal(barrier, inc=1, device_id={"batch": lax.rem(mb + k, nb)}, device_id_type=pl.DeviceIdType.MESH)
    pl.semaphore_signal(barrier, inc=1, device_id={"tp": other}, device_id_type=pl.DeviceIdType.MESH)

    mine = kv.at[me]
    sources = (
        (k_hbm.at[0], mine.at[:, pl.ds(0, kw)]), (v_hbm.at[0], mine.at[:, pl.ds(kw, kw)]), (own_hbm, own_ref),
        (dq_hbm, dq_ref), (dk_hbm, dk_ref), (dv_hbm, dv_ref), (tab_hbm, tab_ref), (len_hbm, len_ref),
        (ck_hbm, ck_ref), (cv_hbm, cv_ref), (q_hbm.at[0], q_vm), (w_hbm, w_vm))
    copies = [pltpu.make_async_copy(a, b, local_sem.at[i]) for i, (a, b) in enumerate(sources)]
    for copy in copies:
        copy.start()
    w_copy = copies.pop()
    q_copy = copies.pop()
    for copy in copies[:3]:
        copy.wait()

    owners = [own_ref[0, 0, j] for j in range(pages)]
    ranks = []
    for j in range(pages):
        rank = jnp.int32(0)
        for i in range(j):
            rank = rank + jnp.where(owners[i] == owners[j], 1, 0)
        ranks.append(rank)
    wide = MOST * page_rows
    source_page = iota((1, tok), 1) // page_rows
    place = jnp.zeros((1, tok), jnp.int32)
    for j in range(pages):
        place = jnp.where(source_page == j, owners[j] * MOST + ranks[j], place)
    row = iota((nb * wide, tok), 0)
    column = iota((nb * wide, tok), 1)
    chosen = (row // page_rows == place) & (row % page_rows == column % page_rows)
    chosen = jnp.where(chosen, 1.0, 0.0).astype(jnp.bfloat16)
    moved = jnp.dot(chosen, kv[me], preferred_element_type=jnp.float32)
    page_send[...] = moved.astype(jnp.bfloat16).reshape(nb, wide, 2 * kw)
    for o in range(nb):
        count = jnp.int32(0)
        for j in range(pages):
            count = count + jnp.where(owners[j] == o, 1, 0)
        count_send[o] = jnp.full((ROWS, LANES), count, jnp.int32)
    page_recv[mb] = page_send[mb]
    count_recv[mb] = count_send[mb]

    pl.semaphore_wait(barrier, (n - 1) + (nb - 1) + 1)

    def ring(i):
        block = me - i
        return pltpu.make_async_remote_copy(
            src_ref=kv.at[block], dst_ref=kv.at[block], send_sem=ring_send.at[i], recv_sem=ring_recv.at[i],
            device_id={"seq": me + 1}, device_id_type=pl.DeviceIdType.MESH)

    def arrival(i):
        block = me - 1 - i
        return pltpu.make_async_remote_copy(
            src_ref=kv.at[block], dst_ref=kv.at[block], send_sem=ring_send.at[i], recv_sem=ring_recv.at[i],
            device_id={"seq": me - 1}, device_id_type=pl.DeviceIdType.MESH)

    def page_pair(k):
        to = lax.rem(mb + k, nb)
        return (
            pltpu.make_async_remote_copy(
                src_ref=count_send.at[to], dst_ref=count_recv.at[mb], send_sem=count_ss.at[k - 1],
                recv_sem=count_rs.at[k - 1], device_id={"batch": to}, device_id_type=pl.DeviceIdType.MESH),
            pltpu.make_async_remote_copy(
                src_ref=page_send.at[to], dst_ref=page_recv.at[mb], send_sem=page_ss.at[k - 1],
                recv_sem=page_rs.at[k - 1], device_id={"batch": to}, device_id_type=pl.DeviceIdType.MESH),
        )

    def page_arrival(k):
        since = lax.rem(mb - k + nb, nb)
        return (
            pltpu.make_async_remote_copy(
                src_ref=count_send.at[since], dst_ref=count_recv.at[since], send_sem=count_ss.at[k - 1],
                recv_sem=count_rs.at[k - 1], device_id={"batch": since}, device_id_type=pl.DeviceIdType.MESH),
            pltpu.make_async_remote_copy(
                src_ref=page_send.at[since], dst_ref=page_recv.at[since], send_sem=page_ss.at[k - 1],
                recv_sem=page_rs.at[k - 1], device_id={"batch": since}, device_id_type=pl.DeviceIdType.MESH),
        )

    even = lax.rem(me, 2) == 0

    def two_up():
        return pltpu.make_async_remote_copy(
            src_ref=kv.at[me], dst_ref=kv.at[me], send_sem=ring_send.at[n - 1], recv_sem=ring_recv.at[1],
            device_id={"seq": me + 2}, device_id_type=pl.DeviceIdType.MESH)

    @pl.when(me < n - 1)
    def _():
        ring(0).start()

    @pl.when(even & (me < n - 2))
    def _():
        two_up().start()

    for k in range(1, nb):
        for copy in page_pair(k):
            copy.start()

    def relay(i):
        @pl.when((me > i) & (me < n - 1) & (even | (i > 0)))
        def _():
            arrival(i).wait_recv()
            ring(i + 1).start()

    def final_arrival(i):
        @pl.when((me > i) & ((me == n - 1) | (~even & (i == 0))))
        def _():
            arrival(i).wait_recv()

    for copy in copies[3:]:
        copy.wait()

    for packed, ref in ((q8, dq_ref), (dk8, dk_ref), (dv8, dv_ref)):
        packed[...] = jnp.zeros_like(packed)
        for m in range(new):
            packed[m * requests:(m + 1) * requests, :] = ref[m]
    per_head = group * ROWS
    diagonal = []
    for a in range(k_heads):
        rows = jnp.concatenate(
            [q8[:, (a * group + g) * HD:(a * group + g + 1) * HD] for g in range(group)], axis=0)
        nothing = jnp.zeros((per_head, HD), jnp.float32)
        diagonal.append(jnp.concatenate([rows if b == a else nothing for b in range(k_heads)], axis=1))
    dec_q = jnp.concatenate(halves(jnp.concatenate(diagonal, axis=0)), axis=0)
    lanes = k_heads * per_head

    def dec_scores(keys):
        both = nt_dot(keys, dec_q)
        return (both[:, :lanes] + both[:, lanes:]) * scaling

    cache_rows = pool * page_rows
    token = iota((1, lanes), 1) % ROWS
    request = token % requests
    score_cache = dec_scores(ck_ref[...].reshape(cache_rows, kw))
    slot_of = iota((cache_rows, lanes), 0) // page_rows
    within = iota((cache_rows, lanes), 0) % page_rows
    live = jnp.zeros((cache_rows, lanes), jnp.int32)
    for r in range(requests):
        for j in range(slots):
            first = (j * n + me) * page_rows
            named = (slot_of == tab_ref[r, j]) & (request == r) & (first + within < len_ref[r])
            live = jnp.where(named, 1, live)
    score_cache = jnp.where(live > 0, score_cache, floor_score)
    new_k = jnp.concatenate([part.astype(jnp.float32) for part in halves(dk8[...])], axis=0).astype(jnp.bfloat16)
    new_v = jnp.concatenate([part.astype(jnp.float32) for part in halves(dv8[...])], axis=0).astype(jnp.bfloat16)
    score_new = dec_scores(new_k)
    score_new = score_new[:ROWS] + score_new[ROWS:]
    key_token = iota((ROWS, lanes), 0)
    causal = (key_token % requests == request) & (key_token <= token) & (me == 0)
    score_new = jnp.where(causal, score_new, floor_score)

    early_peak = jnp.maximum(jnp.max(score_cache, axis=0, keepdims=True), jnp.max(score_new, axis=0, keepdims=True))
    weight_cache = jnp.where(live > 0, jnp.exp(score_cache - early_peak), 0.0)
    weight_new = jnp.where(causal, jnp.exp(score_new - early_peak), 0.0)
    early_total = jnp.sum(weight_cache, axis=0, keepdims=True) + jnp.sum(weight_new, axis=0, keepdims=True)

    def dec_values(values, weights):
        both = tn_dot(values, jnp.concatenate(halves(weights), axis=1))
        return both[:, :lanes] + both[:, lanes:]

    lane_head = iota((HD, lanes), 1) // per_head

    def own_head(mixed):
        acc = mixed[0:HD]
        for a in range(1, k_heads):
            acc = jnp.where(lane_head == a, mixed[a * HD:(a + 1) * HD], acc)
        return acc

    early_acc = own_head(
        dec_values(cv_ref[...].reshape(cache_rows, kw), weight_cache)
        + dec_values(new_v, jnp.concatenate([weight_new, weight_new], axis=0)))

    pair = 2
    pair_lanes = pair * tok
    sharpness = scaling * LOG2E
    visible = iota((tok, pair_lanes), 0) <= iota((tok, pair_lanes), 1) % tok

    def prefill_block(block, first):
        for a in range(k_heads):
            keys = kv[block, :, a * HD:(a + 1) * HD]
            values = kv[block, :, kw + a * HD:kw + (a + 1) * HD].T
            for p in range(group // pair):
                at = a * (group // pair) + p
                queries = jnp.concatenate(
                    [q_vm[:, (at * pair + i) * HD:(at * pair + i + 1) * HD] for i in range(pair)], axis=0)
                scores = nt_dot(keys, queries)
                if first:
                    scores = jnp.where(visible, scores, floor_score)
                high = jnp.max(scores, axis=0, keepdims=True)
                if not first:
                    before = peak_ref[at, 0:1, :]
                    high = jnp.maximum(high, before)
                weights = jnp.exp2((scores - high) * sharpness)
                sums = jnp.sum(weights, axis=0, keepdims=True)
                mixture = jnp.dot(values, weights.astype(jnp.bfloat16), preferred_element_type=jnp.float32)
                if not first:
                    shrink = jnp.exp2((before - high) * sharpness)
                    sums = sums + total_ref[at, 0:1, :] * shrink
                    mixture = mixture + mix_ref[at] * shrink
                peak_ref[at, 0:1, :] = high
                total_ref[at, 0:1, :] = sums
                mix_ref[at] = mixture

    q_copy.wait()
    prefill_block(me, True)
    relay(0)

    for k in range(1, nb):
        for copy in page_arrival(k):
            copy.wait_recv()
    received = page_recv[...].reshape(nb * wide, 2 * kw)
    score_recv = dec_scores(received[:, :kw])
    place_of = iota((wide, lanes), 0) // page_rows
    kept = jnp.concatenate([jnp.where(place_of < count_recv[b][0:1, :], 1, 0) for b in range(nb)], axis=0)
    score_recv = jnp.where(kept > 0, score_recv, floor_score)
    peak = jnp.maximum(early_peak, jnp.max(score_recv, axis=0, keepdims=True))
    weight_recv = jnp.where(kept > 0, jnp.exp(score_recv - peak), 0.0)
    carried = jnp.exp(early_peak - peak)
    total = early_total * carried + jnp.sum(weight_recv, axis=0, keepdims=True)
    acc = early_acc * carried + own_head(dec_values(received[:, kw:], weight_recv))
    acc_all[me] = acc.astype(jnp.bfloat16)
    stat_row = iota((ROWS, lanes), 0)
    stat_all[me] = jnp.where(stat_row == 0, peak, total)

    def partial_pair(k, slot, to):
        return (
            pltpu.make_async_remote_copy(
                src_ref=acc_all.at[slot], dst_ref=acc_all.at[slot], send_sem=acc_ss.at[k - 1],
                recv_sem=acc_rs.at[k - 1], device_id={"seq": to}, device_id_type=pl.DeviceIdType.MESH),
            pltpu.make_async_remote_copy(
                src_ref=stat_all.at[slot], dst_ref=stat_all.at[slot], send_sem=stat_ss.at[k - 1],
                recv_sem=stat_rs.at[k - 1], device_id={"seq": to}, device_id_type=pl.DeviceIdType.MESH),
        )

    for k in range(1, n):
        for copy in partial_pair(k, me, lax.rem(me + k, n)):
            copy.start()

    if n > 2:
        relay(1)
    final_arrival(0)

    @pl.when(me >= 1)
    def _():
        prefill_block(me - 1, False)

    if n > 2:
        final_arrival(1)

        @pl.when(me >= 2)
        def _():
            prefill_block(me - 2, False)

    def finish():
        unit = jnp.where(iota((tok, tok), 0) == iota((tok, tok), 1), 1.0, 0.0).astype(jnp.bfloat16)
        for at in range(q_heads // pair):
            done = (mix_ref[at] * (1.0 / total_ref[at, 0:1, :])).astype(jnp.bfloat16)
            for i in range(pair):
                turned = nt_dot(unit, done[:, i * tok:(i + 1) * tok])
                head = at * pair + i
                out_ref[0, :, head * HD:(head + 1) * HD] = turned.astype(jnp.bfloat16)

    @pl.when(me <= 1)
    def _():
        finish()

    for k in range(1, n):
        since = lax.rem(me - k + n, n)
        for copy in partial_pair(k, since, since):
            copy.wait_recv()
    peaks = [stat_all[s][0:1, :] for s in range(n)]
    top = functools.reduce(jnp.maximum, peaks)
    scales = [jnp.exp(p - top) for p in peaks]
    whole = sum(stat_all[s][1:2, :] * scales[s] for s in range(n))
    merged = sum(acc_all[s].astype(jnp.float32) * scales[s] for s in range(n)) / whole
    merged = merged.T
    attention = jnp.concatenate([merged[h * ROWS:(h + 1) * ROWS] for h in range(q_heads)], axis=1)
    parts = jnp.concatenate([p.astype(jnp.float32) for p in halves(attention)], axis=0).astype(jnp.bfloat16)
    w_copy.wait()
    step = w_vm.shape[1] // w_chunks

    def y_copy(c):
        return pltpu.make_async_remote_copy(
            src_ref=y_send.at[c], dst_ref=y_recv.at[c], send_sem=y_ss.at[c], recv_sem=y_rs.at[c],
            device_id={"tp": other}, device_id_type=pl.DeviceIdType.MESH)

    for c in range(w_chunks):
        both = jnp.dot(parts, w_vm[:, c * step:(c + 1) * step], preferred_element_type=jnp.float32)
        y_send[c] = both[:ROWS] + both[ROWS:]
        y_copy(c).start()

    def later(i, carry):
        @pl.when(me >= i)
        def _():
            arrival(i - 1).wait_recv()

            @pl.when(me < n - 1)
            def _():
                ring(i).start()

            prefill_block(me - i, False)
        return carry

    lax.fori_loop(3, n, later, 0)

    @pl.when(me > 1)
    def _():
        finish()

    for c in range(w_chunks):
        y_copy(c).wait()
        y = y_send[c] + y_recv[c]
        for m in range(new):
            dec_ref[m, :, c * step:(c + 1) * step] = y[m * requests:(m + 1) * requests]

    for i in range(n - 1):
        @pl.when((me < n - 1) & (me >= i) & (even | (i != 1)))
        def _():
            ring(i).wait_send()

    @pl.when(even & (me < n - 2))
    def _():
        two_up().wait_send()
    for k in range(1, nb):
        for copy in page_pair(k):
            copy.wait_send()
    for k in range(1, n):
        for copy in partial_pair(k, me, lax.rem(me + k, n)):
            copy.wait_send()


def hand_over(pre_ref, dec_ref, pre_hbm, dec_hbm, sems):
    copies = [
        pltpu.make_async_copy(a, b, sems.at[i]) for i, (a, b) in enumerate(((pre_ref, pre_hbm), (dec_ref, dec_hbm)))]
    for copy in copies:
        copy.start()
    for copy in copies:
        copy.wait()


def local(
    pre_q, pre_k, pre_v, owner_map, cache_k, cache_v, tables, lengths, dec_q, dec_k, dec_v, w_out
):
    n = lax.axis_size("seq")
    nb = lax.axis_size("batch")
    tok = pre_q.shape[1]
    kw = pre_k.shape[2]
    page_rows = cache_k.shape[1]
    lanes = pre_q.shape[2] // HD * ROWS
    out_columns = w_out.shape[1]
    w_chunks = max(1, out_columns // 512)
    vmem = pl.BlockSpec(memory_space=pltpu.VMEM)
    hbm = pl.BlockSpec(memory_space=pltpu.HBM)
    dma = pltpu.SemaphoreType.DMA
    pre_out, dec_out = pl.pallas_call(
        functools.partial(kernel, n, nb, page_rows, w_chunks),
        out_shape=(
            pltpu.VMEM(pre_q.shape, jnp.bfloat16),
            pltpu.VMEM((dec_q.shape[1], dec_q.shape[0], out_columns), jnp.float32),
        ),
        in_specs=[hbm] * 12,
        out_specs=(vmem, vmem),
        scratch_shapes=[
            pltpu.SMEM((1, 1, owner_map.shape[1]), jnp.int32),
            pltpu.SMEM(tables.shape, jnp.int32),
            pltpu.SMEM(lengths.shape, jnp.int32),
            pltpu.VMEM(cache_k.shape, jnp.bfloat16),
            pltpu.VMEM(cache_v.shape, jnp.bfloat16),
            pltpu.VMEM((dec_q.shape[1], dec_q.shape[0], dec_q.shape[2]), jnp.float32),
            pltpu.VMEM((dec_q.shape[1], dec_q.shape[0], kw), jnp.float32),
            pltpu.VMEM((dec_q.shape[1], dec_q.shape[0], kw), jnp.float32),
            pltpu.VMEM((lanes // (2 * ROWS), HD, 2 * tok), jnp.float32),
            pltpu.VMEM((lanes // (2 * ROWS), ROWS, 2 * tok), jnp.float32),
            pltpu.VMEM((lanes // (2 * ROWS), ROWS, 2 * tok), jnp.float32),
            pltpu.VMEM((n, tok, 2 * kw), jnp.bfloat16),
            pltpu.VMEM((tok, pre_q.shape[2]), jnp.bfloat16),
            pltpu.VMEM(w_out.shape, jnp.bfloat16),
            pltpu.VMEM((nb, MOST * page_rows, 2 * kw), jnp.bfloat16),
            pltpu.VMEM((nb, MOST * page_rows, 2 * kw), jnp.bfloat16),
            pltpu.VMEM((nb, ROWS, LANES), jnp.int32),
            pltpu.VMEM((nb, ROWS, LANES), jnp.int32),
            pltpu.VMEM((n, HD, lanes), jnp.bfloat16),
            pltpu.VMEM((n, ROWS, lanes), jnp.float32),
            pltpu.VMEM((ROWS, dec_q.shape[2]), jnp.float32),
            pltpu.VMEM((ROWS, kw), jnp.float32),
            pltpu.VMEM((ROWS, kw), jnp.float32),
            pltpu.VMEM((w_chunks, ROWS, out_columns // w_chunks), jnp.float32),
            pltpu.VMEM((w_chunks, ROWS, out_columns // w_chunks), jnp.float32),
            dma((12,)),
            dma((n,)), dma((n - 1,)),
            dma((nb - 1,)), dma((nb - 1,)), dma((nb - 1,)), dma((nb - 1,)),
            dma((n - 1,)), dma((n - 1,)), dma((n - 1,)), dma((n - 1,)),
            dma((w_chunks,)), dma((w_chunks,)),
        ],
        compiler_params=pltpu.CompilerParams(
            collective_id=0, has_side_effects=True, vmem_limit_bytes=48 * 1024 * 1024
        ),
        name="prefill_and_decode",
    )(*(pltpu.with_memory_space_constraint(x, pltpu.HBM) for x in (
        jnp.swapaxes(owner_map, 1, 2), tables, lengths, pre_k, pre_v, cache_k, cache_v,
        *(jnp.swapaxes(x, 0, 1) for x in (dec_q, dec_k, dec_v)), pre_q, w_out,
    )))
    pre_out, dec_out = pl.pallas_call(
        hand_over,
        out_shape=(pltpu.HBM(pre_out.shape, pre_out.dtype), pltpu.HBM(dec_out.shape, dec_out.dtype)),
        in_specs=[vmem] * 2,
        out_specs=(hbm, hbm),
        scratch_shapes=[dma((2,))],
        name="hand_over",
    )(*(pltpu.with_memory_space_constraint(x, pltpu.VMEM) for x in (pre_out, dec_out)))
    return pre_out, jnp.swapaxes(dec_out, 0, 1)


def solution(mesh):
    placed = (
        P("batch", "seq", "tp"),
        P("batch", "seq", "tp"),
        P("batch", "seq", "tp"),
        P("batch", "seq", None),
        P("batch", "seq", "tp"),
        P("batch", "seq", "tp"),
        P("batch", "seq"),
        P("batch"),
        P("batch", None, "tp"),
        P("batch", None, "tp"),
        P("batch", None, "tp"),
        P("tp", "seq"),
    )
    return jax.shard_map(
        local,
        mesh=mesh,
        in_specs=placed,
        out_specs=(P("batch", "seq", "tp"), P("batch", None, "seq")),
        check_vma=False,
    )
```
